256 devices in a mesh: node: 32 (over z, x_lo, core), local: 8 (over x_hi, y).
Axes of the slice: x: 4 (x_hi: 2, x_lo: 2; x = x_hi * 2 + x_lo), y: 4, z: 8, core: 2. Of those that a mesh axis runs over, the one named last changes fastest.
Arguments:
- tokens: bfloat16 [4096, 10240], P('node'), may hold values from -6 to 6
- master: float32 [10240, 10240], P('node', 'local'), may hold values from -0.0625 to 0.0625
- moment_one: float32 [10240, 10240], P('node', 'local'), may hold values from -6 to 6
- moment_two: float32 [10240, 10240], P('node', 'local'), may hold values from 0.5 to 20
- keys: bfloat16 [4096, 1024], P('node', 'local'), may hold values from -60 to 60
- values: bfloat16 [4096, 1024], P('node', 'local'), may hold values from -6 to 6
- d_context: bfloat16 [4096, 10240], P('node', 'local'), may hold values from -6 to 6
Outputs:
- context: bfloat16 [4096, 10240], P('node', 'local')
- d_keys: bfloat16 [4096, 1024], P('node', 'local')
- d_values: bfloat16 [4096, 1024], P('node', 'local')
- d_tokens: bfloat16 [4096, 10240], P(('node', 'local'))
- new_master: float32 [10240, 10240], P('node', 'local')
- new_moment_one: float32 [10240, 10240], P('node', 'local')
- new_moment_two: float32 [10240, 10240], P('node', 'local')
The draws below stay inside these ranges and needn't reach their ends.
All inputs are finite; a program needn't handle non-finite values.
Results may differ from the reference program's by a relative error of at most 0.04.
The reference program's roundings to bfloat16 on the way (of `weight`, `queries`, `probs_low`, `d_scores` and `d_queries`) count: a program that leaves them out, or rounds other values in their place, can miss the bound.
Values may be sent and summed in bfloat16 or wider, within the bound.
A program may use at most 192 MiB of HBM per device.

```python
import math
import jax
import jax.numpy as jnp
from jax import lax

D = 10240
HS = 128
HEADS_DEV = 10
TOK_NODE = 128
HEADS = 80
KV_HEADS = 8
TOKENS = 4096
N_NODE = 32
N_LOCAL = 8


def draw_keys(key, part):
    key = jax.random.fold_in(key, 7)
    first = jax.random.fold_in(key, 0)
    base = jax.random.normal(first, (TOKENS, KV_HEADS * HS), jnp.float32)
    return jnp.clip(base, -4.0, 4.0).astype(jnp.bfloat16)


def level_of(rng, extent, cuts, least, top_value):
    factor_of, own = 1.0, jax.random.fold_in(rng, 6)
    for dim, parts in cuts:
        steps = jnp.exp(jax.random.uniform(jax.random.fold_in(own, dim), (parts,), jnp.float32, least / len(cuts), top_value / len(cuts)))
        factor_of = factor_of * jnp.repeat(steps, extent[dim] // parts).reshape([-1 if axis == dim else 1 for axis in range(len(extent))])
    return factor_of


def noise(rng, shape, width, limit, shards=(), held_as=jnp.bfloat16):
    values = jax.random.normal(rng, shape, jnp.float32) * width
    if len(shards) > 0:
        values = level_of(rng, shape, shards, -0.22, 0.18) * values
    return jnp.clip(values, min=-limit, max=limit).astype(held_as)


def setup_inputs(seed: int = 0) -> dict:
    splits = jax.random.split(jax.random.key(seed), 8)
    tokens = noise(splits[0], (TOKENS, D), 1.0, 6.0, ((0, 32),))
    master = noise(splits[1], (D, HEADS * HS), D ** -0.5, 0.0625, ((0, 32), (1, 8)), jnp.float32)
    moment_one = noise(splits[2], (D, HEADS * HS), 1.0, 6.0, ((0, 32), (1, 8)), jnp.float32)
    moment_two = jnp.clip(jnp.exp(math.log(20.0) - 3.6888795 * jax.random.uniform(splits[3], (D, HEADS * HS), jnp.float32) ** level_of(splits[3], (D, HEADS * HS), ((0, 32), (1, 8)), -0.2, 0.2)), 0.5, 20.0)
    keys = draw_keys(jax.random.fold_in(splits[7], 71), 0)
    values = noise(splits[5], (TOKENS, KV_HEADS * HS), 1.0, 6.0, ((0, 32), (1, 8)))
    d_context = noise(splits[6], (TOKENS, HEADS * HS), 1.0, 6.0, ((0, 32), (1, 8)))
    return {"tokens": tokens, "master": master, "moment_one": moment_one, "moment_two": moment_two, "keys": keys, "values": values, "d_context": d_context}


def attend(pieces):
    query_seq, key_seq, value_seq, grad_seq = pieces
    length = query_seq.shape[0]
    scale = 1.0 / HS ** 0.5
    key_wide = jnp.repeat(key_seq, HEADS_DEV, axis=1).astype(jnp.float32)
    value_wide = jnp.repeat(value_seq, HEADS_DEV, axis=1).astype(jnp.float32)
    query_wide = query_seq.astype(jnp.float32)
    grad_wide = grad_seq.astype(jnp.float32)
    scores = jnp.einsum('qhd,khd->hqk', query_wide, key_wide) * scale
    rows_idx = lax.broadcasted_iota(jnp.int32, (length, length), 0)
    cols_idx = lax.broadcasted_iota(jnp.int32, (length, length), 1)
    scores = jnp.where((cols_idx <= rows_idx)[None], scores, jnp.float32(-1e+30))
    probs = jax.nn.softmax(scores, axis=-1)
    probs_low = probs.astype(jnp.bfloat16)
    context = jnp.einsum('hqk,khd->qhd', probs_low.astype(jnp.float32), value_wide).astype(jnp.bfloat16)
    d_probs = jnp.einsum('qhd,khd->hqk', grad_wide, value_wide)
    inner = lax.optimization_barrier(jnp.sum(d_probs * probs, axis=-1, keepdims=True))
    d_scores = (probs * (d_probs - inner) * scale).astype(jnp.bfloat16)
    d_scores_wide = d_scores.astype(jnp.float32)
    dv_heads = jnp.einsum('hqk,qhd->khd', probs_low.astype(jnp.float32), grad_wide)
    dk_heads = jnp.einsum('hqk,qhd->khd', d_scores_wide, query_wide)
    groups = key_seq.shape[1]
    d_values = dv_heads.reshape(length, groups, HEADS_DEV, HS).sum(axis=2).astype(jnp.bfloat16)
    d_keys = dk_heads.reshape(length, groups, HEADS_DEV, HS).sum(axis=2).astype(jnp.bfloat16)
    d_queries = jnp.einsum('hqk,khd->qhd', d_scores_wide, key_wide).astype(jnp.bfloat16)
    return (context, d_keys, d_values, d_queries)

def reference(tokens, master, moment_one, moment_two, keys, values, d_context):
    weight = master.astype(jnp.bfloat16)
    queries = jnp.dot(tokens, weight, preferred_element_type=jnp.float32).astype(jnp.bfloat16)
    query_seqs = queries.reshape(N_NODE, TOK_NODE, HEADS, HS)
    key_seqs = keys.reshape(N_NODE, TOK_NODE, KV_HEADS, HS)
    value_seqs = values.reshape(N_NODE, TOK_NODE, KV_HEADS, HS)
    grad_seqs = d_context.reshape(N_NODE, TOK_NODE, HEADS, HS)
    context, d_keys, d_values, d_queries = lax.map(attend, (query_seqs, key_seqs, value_seqs, grad_seqs))
    context = context.reshape(TOKENS, HEADS * HS)
    d_keys = d_keys.reshape(TOKENS, KV_HEADS * HS)
    d_values = d_values.reshape(TOKENS, KV_HEADS * HS)
    d_queries = d_queries.reshape(TOKENS, HEADS * HS)
    group_cols = HEADS_DEV * HS

    def add_group(index, total):
        start = (index * group_cols).astype(jnp.int32)
        grad_block = lax.dynamic_slice_in_dim(d_queries, start, group_cols, 1)
        weight_block = lax.dynamic_slice_in_dim(weight, start, group_cols, 1)
        part = lax.dot_general(grad_block, weight_block, (((1,), (1,)), ((), ())), preferred_element_type=jnp.float32)
        return total + part.astype(jnp.bfloat16).astype(jnp.float32)
    d_tokens = lax.fori_loop(0, N_LOCAL, add_group, jnp.zeros((TOKENS, D), jnp.float32)).astype(jnp.bfloat16)

    def add_seq(index, total):
        start = (index * TOK_NODE).astype(jnp.int32)
        token_block = lax.dynamic_slice_in_dim(tokens, start, TOK_NODE, 0)
        grad_block = lax.dynamic_slice_in_dim(d_queries, start, TOK_NODE, 0)
        part = lax.dot_general(token_block, grad_block, (((0,), (0,)), ((), ())), preferred_element_type=jnp.float32)
        return total + part.astype(jnp.bfloat16).astype(jnp.float32)
    gradient = lax.fori_loop(0, N_NODE, add_seq, jnp.zeros((D, HEADS * HS), jnp.float32))
    new_moment_one = 0.9 * moment_one + 0.1 * gradient
    new_moment_two = 0.999 * moment_two + 0.001 * gradient * gradient
    first_hat = new_moment_one / (1.0 - 0.9 ** 10)
    second_hat = new_moment_two / (1.0 - 0.999 ** 10)
    new_master = master - 0.001 * first_hat / (jnp.sqrt(second_hat) + 1e-08)
    return (context, d_keys, d_values, d_tokens, new_master, new_moment_one, new_moment_two)
```

```python
import functools

import jax
import jax.numpy as jnp
from jax import lax
from jax.experimental import pallas as pl
from jax.experimental.pallas import tpu as pltpu
from jax.sharding import PartitionSpec as P

MESH = pl.DeviceIdType.MESH
HS = 128
NZ, NY = 8, 4
PW = 2 * HS
ORDER = (4, 3, 5, 2, 6, 1, 7)
F32, BF16 = jnp.float32, jnp.bfloat16


def adam_piece(master, moment_one, moment_two, gradient):
    new_one = 0.9 * moment_one + 0.1 * gradient
    new_two = 0.999 * moment_two + 0.001 * gradient * gradient
    first_hat = new_one / (1.0 - 0.9**10)
    second_hat = new_two / (1.0 - 0.999**10)
    new_master = master - 0.001 * first_hat / (jnp.sqrt(second_hat) + 1e-08)
    return (new_master, new_one, new_two)


def dot(a, b, dims=((1,), (0,))):
    return lax.dot_general(a, b, (dims, ((), ())), preferred_element_type=F32)


def kernel(
    tokens_ref, master_ref, keys_ref, values_ref, dctx_ref,
    ctx_ref, dk_ref, dv_ref, dtok_ref, grad_ref,
    tok, tok_t, wg, part, ring, dqall, dk_acc, dv_acc, dacc, dts, yr2, yr1, red, xr, fin, dtk,
    ga, gs, gcr, gxs, gxr,
    own_sem, w_s, w_r, tz_s, tz_r, ty_s, ty_r, rs_s, rs_r, ag_s, ag_r, y_s, y_r, x_s, x_r, zd_s, zd_r,
    gc_s, gc_r, gx_s, gx_r,
):
    length = keys_ref.shape[0]
    rows, cols = master_ref.shape
    depth = 4 * rows
    pairs = cols // PW
    node, local = lax.axis_index("node"), lax.axis_index("local")
    z, r = node // 4, node % 4
    xl, c = r // 2, r % 2
    xh, y = local // NY, local % NY
    quarter = length // NY
    half_rows = quarter // 2

    def plane(offset):
        return (z + offset + NZ) % NZ

    def at_z(where):
        return {"node": where * 4 + r, "local": local}

    def at_y(where):
        return {"node": node, "local": xh * NY + where}

    z_up, z_dn = at_z(plane(1)), at_z(plane(-1))
    yp, ym, y2 = (y + 1) % NY, (y + 3) % NY, (y + 2) % NY
    y_up, y_dn = at_y(yp), at_y(ym)
    other_core = {"node": z * 4 + xl * 2 + (1 - c), "local": local}
    other_xl = {"node": z * 4 + (1 - xl) * 2 + c, "local": local}
    other_xh = {"node": node, "local": (1 - xh) * NY + y}

    def remote(src, dst, send_sem, recv_sem, device):
        return pltpu.make_async_remote_copy(
            src_ref=src, dst_ref=dst, send_sem=send_sem, recv_sem=recv_sem,
            device_id=device, device_id_type=MESH,
        )

    barrier = pltpu.get_barrier_semaphore()
    partners = [at_z(plane(d)) for d in range(1, NZ)] + [y_up, y_dn, other_core, other_xl, other_xh]
    for device in partners:
        pl.semaphore_signal(barrier, inc=1, device_id=device, device_id_type=MESH)
    pl.semaphore_wait(barrier, len(partners))

    def row_block(base, count):
        return pl.ds(pl.multiple_of(base, 16), count)

    def token_out(j):
        to = plane(ORDER[j])
        src = tokens_ref.at[row_block(y * quarter, quarter), pl.ds(pl.multiple_of(to * depth, 128), depth)]
        return remote(src, tok.at[z, row_block(y * quarter, quarter), :], tz_s.at[j], tz_r.at[j], at_z(to))

    def token_in(j):
        block = tok.at[plane(-ORDER[j]), row_block(y * quarter, quarter), :]
        return remote(block, block, tz_s.at[j], tz_r.at[j], z_up)

    def token_y(j, kind, incoming):
        s = plane(-ORDER[j])
        me = (yp if kind in (1, 3) else ym) if incoming else y
        base, count = me * quarter, quarter
        if kind >= 2:
            origin = y2 if incoming else (ym if kind == 2 else yp)
            base, count = origin * quarter + (0 if kind == 2 else half_rows), half_rows
        block = tok.at[s, row_block(base, count), :]
        return remote(block, block, ty_s.at[kind, j], ty_r.at[kind, j], y_up if kind in (0, 2) else y_dn)

    for j in range(NZ - 1):
        token_out(j).start()
    own_tokens = pltpu.make_async_copy(
        tokens_ref.at[:, pl.ds(pl.multiple_of(z * depth, 128), depth)], tok.at[z], own_sem
    )
    own_tokens.start()

    def w_block(k, which):
        return wg.at[k, pl.ds(pl.multiple_of(which * rows, 64), rows), :]

    def w_copy(kind, k, incoming):
        sent = (r, r, r ^ 2)[kind]
        came = (r ^ 1, r ^ 2, r ^ 3)[kind]
        block = w_block(k, came if incoming else sent)
        return remote(block, block, w_s.at[kind, k], w_r.at[kind, k], other_xl if kind == 1 else other_core)

    for k in range(pairs):
        wg[k, pl.ds(pl.multiple_of(r * rows, 64), rows), :] = master_ref[:, k * PW : (k + 1) * PW].astype(BF16)
        w_copy(1, k, False).start()
        w_copy(0, k, False).start()

    def hand_on(j):
        token_y(j, 0, True).wait_recv()
        token_y(j, 2, False).start()
        token_y(j, 1, True).wait_recv()
        token_y(j, 3, False).start()

    for j in range(NZ - 1):
        token_in(j).wait_recv()
        token_y(j, 0, False).start()
        token_y(j, 1, False).start()
        if j < pairs:
            w_copy(1, j, True).wait_recv()
            w_copy(2, j, False).start()
        if j >= 1:
            hand_on(j - 1)
    hand_on(NZ - 2)
    own_tokens.wait()
    for j in range(NZ - 1):
        token_y(j, 2, True).wait_recv()
        token_y(j, 3, True).wait_recv()

    def rs_copy(way, d, k):
        sign = 1 if way == 0 else -1
        src = part.at[k, plane(sign * d)]
        dst = ring.at[way, d - 1, k]
        if d == 4:
            src, dst = src.at[way], dst.at[way]
        return remote(src, dst, rs_s.at[way, d - 1, k], rs_r.at[way, d - 1, k], z_up if way == 0 else z_dn)

    def gemm_step(k, carry):
        w_copy(0, k, True).wait_recv()
        w_copy(2, k, True).wait_recv()
        out = dot(tok[...].reshape(NZ * length, depth), wg[k])
        for t in range(NZ):
            for a in range(2):
                part[k, t, a] = out[t * length : (t + 1) * length, a * HS : (a + 1) * HS]
        for way in range(2):
            rs_copy(way, 4, k).start()
        return carry

    lax.fori_loop(0, pairs, gemm_step, 0)
    for d in (3, 2, 1):

        def ring_step(k, carry, d=d):
            for way in range(2):
                rs_copy(way, d + 1, k).wait_recv()
                t = plane(d if way == 0 else -d)
                if d == 3:
                    part[k, t, way] += ring[way, d, k, way]
                else:
                    part[k, t] += ring[way, d, k]
                rs_copy(way, d, k).start()
            return carry

        lax.fori_loop(0, pairs, ring_step, 0)

    def transpose_step(s, carry):
        tok_t[:, pl.ds(pl.multiple_of(s * length, 128), length)] = tok[s].T
        return carry

    lax.fori_loop(0, NZ, transpose_step, 0)

    scale = 1.0 / HS**0.5
    row_id = lax.broadcasted_iota(jnp.int32, (length, length), 0)
    col_id = lax.broadcasted_iota(jnp.int32, (length, length), 1)
    causal = col_id <= row_id
    dk_acc[...] = jnp.zeros_like(dk_acc)
    dv_acc[...] = jnp.zeros_like(dv_acc)

    def ag_copy(way, d, k, incoming):
        sign = -1 if way == 0 else 1
        block = dqall.at[k, plane(sign * (d if incoming else d - 1))]
        if d == 4:
            block = block.at[:, pl.ds(way * HS, HS)]
        return remote(block, block, ag_s.at[way, d - 1, k], ag_r.at[way, d - 1, k], z_up if way == 0 else z_dn)

    def attention_step(k, carry):
        for way in range(2):
            rs_copy(way, 1, k).wait_recv()
        keys, values = keys_ref[...], values_ref[...]
        lanes = pl.ds(pl.multiple_of(k * PW, 128), PW)
        grads = dctx_ref[:, lanes]
        ctx, dq = [], []
        dk, dv = dk_acc[...], dv_acc[...]
        for a in range(2):
            q = (part[k, z, a] + ring[0, 0, k, a] + ring[1, 0, k, a]).astype(BF16)
            g = grads[:, a * HS : (a + 1) * HS]
            scores = jnp.where(causal, dot(q, keys, ((1,), (1,))) * scale, -1e30)
            e = jnp.exp(scores - jnp.max(scores, axis=-1, keepdims=True))
            probs = e * (1.0 / jnp.sum(e, axis=-1, keepdims=True))
            low = probs.astype(BF16)
            ctx.append(dot(low, values).astype(BF16))
            d_probs = dot(g, values, ((1,), (1,)))
            inner = jnp.sum(d_probs * probs, axis=-1, keepdims=True)
            ds = (probs * (d_probs - inner) * scale).astype(BF16)
            dv = dv + dot(low, g, ((0,), (0,)))
            dk = dk + dot(ds, q, ((0,), (0,)))
            dq.append(dot(ds, keys).astype(BF16))
        dk_acc[...], dv_acc[...] = dk, dv
        ctx_ref[:, lanes] = jnp.concatenate(ctx, axis=1)
        dqall[k, z] = jnp.concatenate(dq, axis=1)
        for way in range(2):
            ag_copy(way, 1, k, False).start()
        return carry

    lax.fori_loop(0, pairs, attention_step, 0)
    dk_ref[...] = dk_acc[...].astype(BF16)
    dv_ref[...] = dv_acc[...].astype(BF16)

    groups = [(0, 1), (1, 2), (3, 2), (5, 2), (7, 1)]
    offsets = (0, -1, 1, -2, 2, -3, 3, 4)
    mid = cols // 2

    def y_copy(g, way, d):
        first, count = groups[g]
        slots = pl.ds(first, count)
        if d == 2:
            src = dts.at[slots, y2, :, pl.ds(way * mid, mid)]
            dst = yr2.at[way, slots]
        else:
            src = dts.at[slots, yp if way == 0 else ym]
            dst = yr1.at[way, slots]
        return remote(src, dst, y_s.at[way, d - 1, g], y_r.at[way, d - 1, g], y_up if way == 0 else y_dn)

    def accumulate(g, k):
        first, count = groups[g]
        lhs = jnp.concatenate([dqall[k, plane(offsets[first + i])] for i in range(count)], axis=0)
        return dot(lhs, wg[k], ((1,), (1,)))

    def gemm_out(g, total):
        first, count = groups[g]
        for i in range(count):
            for owner in range(2 * NY):
                block = total[i * length + owner * 16 : i * length + (owner + 1) * 16]
                dts[first + i, owner % NY, (owner // NY) * 16 : (owner // NY + 1) * 16] = block.astype(BF16)
        for way in range(2):
            y_copy(g, way, 2).start()

    def y_first(g):
        first, count = groups[g]
        for way in range(2):
            y_copy(g, way, 2).wait_recv()
            to = yp if way == 0 else ym
            for i in range(count):
                own = dts[first + i, to, :, way * mid : (way + 1) * mid].astype(F32)
                came = yr2[way, first + i].astype(F32)
                dts[first + i, to, :, way * mid : (way + 1) * mid] = (own + came).astype(BF16)
            y_copy(g, way, 1).start()

    def x_copy(g):
        first, count = groups[g]
        slots = pl.ds(first, count)
        return remote(red.at[slots, 1 - xh], xr.at[slots], x_s.at[g], x_r.at[g], other_xh)

    def y_second(g):
        first, count = groups[g]
        for way in range(2):
            y_copy(g, way, 1).wait_recv()
        for i in range(count):
            slot = first + i
            total = dts[slot, y].astype(F32) + yr1[0, slot].astype(F32) + yr1[1, slot].astype(F32)
            for side in range(2):
                red[slot, side] = total[side * 16 : (side + 1) * 16].astype(BF16)
        x_copy(g).start()

    def home_copy(slot):
        block = dtk.at[:, pl.ds(pl.multiple_of(z * depth, 128), depth)]
        return remote(fin.at[slot], block, zd_s.at[slot], zd_r.at[slot], at_z(plane(offsets[slot])))

    def home_in(slot):
        block = dtk.at[:, pl.ds(pl.multiple_of(plane(-offsets[slot]) * depth, 128), depth)]
        return remote(fin.at[slot], block, zd_s.at[slot], zd_r.at[slot], z_up)

    def x_done(g):
        first, count = groups[g]
        x_copy(g).wait_recv()
        for i in range(count):
            slot = first + i
            total = (red[slot, xh].astype(F32) + xr[slot].astype(F32)).astype(BF16)
            if slot == 0:
                dtk[:, pl.ds(pl.multiple_of(z * depth, 128), depth)] = total
            else:
                fin[slot] = total
                home_copy(slot).start()

    dacc[...] = jnp.zeros_like(dacc)

    def own_step(k, carry):
        dacc[:length] += accumulate(0, k)
        return carry

    lax.fori_loop(0, pairs, own_step, 0)
    gemm_out(0, dacc[:length])
    for d in (1, 2, 3):
        dacc[...] = jnp.zeros_like(dacc)

        def gather_step(k, carry, d=d):
            for way in range(2):
                ag_copy(way, d, k, True).wait_recv()
                ag_copy(way, d + 1, k, False).start()
            dacc[...] += accumulate(d, k)
            return carry

        lax.fori_loop(0, pairs, gather_step, 0)
        gemm_out(d, dacc[...])
        y_first(d - 1)
        if d >= 2:
            y_second(d - 2)
        if d >= 3:
            x_done(d - 3)

    def gc_copy(k):
        return remote(gs.at[k], gcr.at[k], gc_s.at[k], gc_r.at[k], other_core)

    def gx_copy(k):
        return remote(gxs.at[k], gxr.at[k], gx_s.at[k], gx_r.at[k], other_xl)

    def own_rows(side, core):
        return pl.ds(pl.multiple_of((side * 2 + core) * rows, 64), rows)

    def core_sum(k):
        gc_copy(k).wait_recv()
        away = 1 - xl
        gxs[k] = (ga[k, own_rows(away, c), :] + gcr[k, away].astype(F32)).astype(BF16)
        gx_copy(k).start()

    def grad_step(k, carry):
        for way in range(2):
            ag_copy(way, 4, k, True).wait_recv()
        ga[k] = dot(tok_t[...], dqall[k].reshape(NZ * length, PW))
        for side in range(2):
            gs[k, side] = ga[k, own_rows(side, 1 - c), :].astype(BF16)
        gc_copy(k).start()

        @pl.when(k >= 1)
        def _():
            core_sum(k - 1)

        return carry

    lax.fori_loop(0, pairs, grad_step, 0)
    core_sum(pairs - 1)

    dacc[...] = jnp.zeros_like(dacc)

    def last_step(k, carry):
        dacc[:length] += accumulate(4, k)
        return carry

    lax.fori_loop(0, pairs, last_step, 0)
    gemm_out(4, dacc[:length])
    y_first(3)
    y_second(2)
    x_done(1)
    y_first(4)
    y_second(3)
    x_done(2)
    y_second(4)
    x_done(3)
    x_done(4)

    for k in range(pairs):
        gx_copy(k).wait_recv()
        mine = ga[k, own_rows(xl, c), :] + gcr[k, xl].astype(F32) + gxr[k].astype(F32)
        grad_ref[:, k * PW : (k + 1) * PW] = mine
    for slot in range(1, NZ):
        home_in(slot).wait_recv()
    dtok_ref[...] = dtk[...]

    for j in range(NZ - 1):
        token_out(j).wait_send()
        for kind in range(4):
            token_y(j, kind, False).wait_send()

    def drain(k, carry):
        for kind in range(3):
            w_copy(kind, k, False).wait_send()
        for way in range(2):
            for d in range(1, 5):
                rs_copy(way, d, k).wait_send()
                ag_copy(way, d, k, False).wait_send()
        gc_copy(k).wait_send()
        gx_copy(k).wait_send()
        return carry

    lax.fori_loop(0, pairs, drain, 0)
    for g in range(len(groups)):
        for way in range(2):
            for d in (1, 2):
                y_copy(g, way, d).wait_send()
        x_copy(g).wait_send()
    for slot in range(1, NZ):
        home_copy(slot).wait_send()


def fused(tokens, master, keys, values, d_context):
    length, width = tokens.shape
    rows, cols = master.shape
    depth, pairs, mid, quarter = 4 * rows, cols // PW, cols // 2, length // NY
    vmem, dma = pltpu.VMEM, pltpu.SemaphoreType.DMA
    in_vmem = pl.BlockSpec(memory_space=pltpu.VMEM)
    return pl.pallas_call(
        kernel,
        out_shape=(
            jax.ShapeDtypeStruct((length, cols), BF16),
            jax.ShapeDtypeStruct((length, HS), BF16),
            jax.ShapeDtypeStruct((length, HS), BF16),
            jax.ShapeDtypeStruct((length // 8, width), BF16),
            jax.ShapeDtypeStruct((rows, cols), F32),
        ),
        in_specs=[pl.BlockSpec(memory_space=pl.ANY)] + [in_vmem] * 4,
        out_specs=[in_vmem] * 5,
        scratch_shapes=[
            vmem((NZ, length, depth), BF16),
            vmem((depth, NZ * length), BF16),
            vmem((pairs, depth, PW), BF16),
            vmem((pairs, NZ, 2, length, HS), F32),
            vmem((2, 4, pairs, 2, length, HS), F32),
            vmem((pairs, NZ, length, PW), BF16),
            vmem((length, HS), F32),
            vmem((length, HS), F32),
            vmem((2 * length, depth), F32),
            vmem((NZ, NY, quarter, depth), BF16),
            vmem((2, NZ, quarter, mid), BF16),
            vmem((2, NZ, quarter, depth), BF16),
            vmem((NZ, 2, 16, depth), BF16),
            vmem((NZ, 16, depth), BF16),
            vmem((NZ, 16, depth), BF16),
            vmem((length // 8, width), BF16),
            vmem((pairs, depth, PW), F32),
            vmem((pairs, 2, rows, PW), BF16),
            vmem((pairs, 2, rows, PW), BF16),
            vmem((pairs, rows, PW), BF16),
            vmem((pairs, rows, PW), BF16),
            dma,
            dma((3, pairs)), dma((3, pairs)),
            dma((NZ - 1,)), dma((NZ - 1,)),
            dma((4, NZ - 1)), dma((4, NZ - 1)),
            dma((2, 4, pairs)), dma((2, 4, pairs)),
            dma((2, 4, pairs)), dma((2, 4, pairs)),
            dma((2, 2, 5)), dma((2, 2, 5)),
            dma((5,)), dma((5,)),
            dma((NZ,)), dma((NZ,)),
            dma((pairs,)), dma((pairs,)),
            dma((pairs,)), dma((pairs,)),
        ],
        compiler_params=pltpu.CompilerParams(
            collective_id=0, has_side_effects=True, vmem_limit_bytes=60 * 1024 * 1024
        ),
    )(tokens, master, keys, values, d_context)


def body(tokens, master, moment_one, moment_two, keys, values, d_context):
    context, d_keys, d_values, d_tokens, gradient = fused(tokens, master, keys, values, d_context)
    new_master, new_one, new_two = adam_piece(master, moment_one, moment_two, gradient)
    return (context, d_keys, d_values, d_tokens, new_master, new_one, new_two)


def solution(mesh):
    both = P("node", "local")
    return jax.shard_map(
        body,
        mesh=mesh,
        in_specs=(P("node", None), both, both, both, both, both, both),
        out_specs=(both, both, both, P(("node", "local"), None), both, both, both),
        check_vma=False,
    )
```

```python
import functools

import jax
import jax.numpy as jnp
from jax import lax
from jax.experimental import pallas as pl
from jax.experimental.pallas import tpu as pltpu
from jax.sharding import PartitionSpec as P

MESH = pl.DeviceIdType.MESH
HS = 128
NZ, NY = 8, 4
PW = 2 * HS
ORDER = (4, 3, 5, 2, 6, 1, 7)
F32, BF16 = jnp.float32, jnp.bfloat16


def adam_piece(master, moment_one, moment_two, gradient):
    new_one = 0.9 * moment_one + 0.1 * gradient
    new_two = 0.999 * moment_two + 0.001 * gradient * gradient
    first_hat = new_one / (1.0 - 0.9**10)
    second_hat = new_two / (1.0 - 0.999**10)
    new_master = master - 0.001 * first_hat / (jnp.sqrt(second_hat) + 1e-08)
    return (new_master, new_one, new_two)


def dot(a, b, dims=((1,), (0,))):
    return lax.dot_general(a, b, (dims, ((), ())), preferred_element_type=F32)


def kernel(
    tokens_hbm, master_hbm, keys_hbm, values_hbm, dctx_hbm,
    ctx_hbm, dk_hbm, dv_hbm, dtok_hbm, grad_hbm,
    master_ref, keys_ref, values_ref, dctx_ref, ctx_ref, dk_ref, dv_ref, grad_ref,
    tok, tok_t, wg, wg_t, part, ring, dqall, dk_acc, dv_acc, d_probs_ref, low_ref, ds_ref, q_ref,
    dts, yr2, yr1, red, xr, fin, dtk,
    ga, gs, gcr, gxs, gxr,
    in_sem, out_sem, own_sem, w_s, w_r, tz_s, tz_r, ty_s, ty_r, rs_s, rs_r, ag_s, ag_r, y_s, y_r, x_s, x_r, zd_s, zd_r,
    gc_s, gc_r, gx_s, gx_r,
):
    length = keys_ref.shape[0]
    rows, cols = master_ref.shape
    depth = 4 * rows
    pairs = cols // PW
    node, local = lax.axis_index("node"), lax.axis_index("local")
    z, r = node // 4, node % 4
    xl, c = r // 2, r % 2
    xh, y = local // NY, local % NY
    quarter = length // NY
    half_rows = quarter // 2

    def plane(offset):
        return (z + offset + NZ) % NZ

    def at_z(where):
        return {"node": where * 4 + r, "local": local}

    def at_y(where):
        return {"node": node, "local": xh * NY + where}

    z_up, z_dn = at_z(plane(1)), at_z(plane(-1))
    yp, ym, y2 = (y + 1) % NY, (y + 3) % NY, (y + 2) % NY
    y_up, y_dn = at_y(yp), at_y(ym)
    other_core = {"node": z * 4 + xl * 2 + (1 - c), "local": local}
    other_xl = {"node": z * 4 + (1 - xl) * 2 + c, "local": local}
    other_xh = {"node": node, "local": (1 - xh) * NY + y}

    def remote(src, dst, send_sem, recv_sem, device):
        return pltpu.make_async_remote_copy(
            src_ref=src, dst_ref=dst, send_sem=send_sem, recv_sem=recv_sem,
            device_id=device, device_id_type=MESH,
        )

    barrier = pltpu.get_barrier_semaphore()
    partners = [at_z(plane(d)) for d in range(1, NZ)] + [y_up, y_dn, other_core, other_xl, other_xh]
    for device in partners:
        pl.semaphore_signal(barrier, inc=1, device_id=device, device_id_type=MESH)
    held = ((master_hbm, master_ref), (keys_hbm, keys_ref), (values_hbm, values_ref), (dctx_hbm, dctx_ref))
    loads = [pltpu.make_async_copy(src, dst, in_sem.at[i]) for i, (src, dst) in enumerate(held)]
    for load in loads:
        load.start()
    own_tokens = pltpu.make_async_copy(
        tokens_hbm.at[:, pl.ds(pl.multiple_of(z * depth, 128), depth)], tok.at[z], own_sem
    )
    own_tokens.start()
    loads[0].wait()
    for k in range(pairs):
        wg[k, pl.ds(pl.multiple_of(r * rows, 64), rows), :] = master_ref[:, k * PW : (k + 1) * PW].astype(BF16)
    pl.semaphore_wait(barrier, len(partners))

    def row_block(base, count):
        return pl.ds(pl.multiple_of(base, 16), count)

    def token_out(j):
        to = plane(ORDER[j])
        src = tokens_hbm.at[row_block(y * quarter, quarter), pl.ds(pl.multiple_of(to * depth, 128), depth)]
        return remote(src, tok.at[z, row_block(y * quarter, quarter), :], tz_s.at[j], tz_r.at[j], at_z(to))

    def token_in(j):
        block = tok.at[plane(-ORDER[j]), row_block(y * quarter, quarter), :]
        return remote(block, block, tz_s.at[j], tz_r.at[j], z_up)

    def token_y(j, kind, incoming):
        s = plane(-ORDER[j])
        me = (yp if kind in (1, 3) else ym) if incoming else y
        base, count = me * quarter, quarter
        if kind >= 2:
            origin = y2 if incoming else (ym if kind == 2 else yp)
            base, count = origin * quarter + (0 if kind == 2 else half_rows), half_rows
        block = tok.at[s, row_block(base, count), :]
        return remote(block, block, ty_s.at[kind], ty_r.at[kind, j], y_up if kind in (0, 2) else y_dn)

    token_out(0).start()
    token_out(2).start()

    def token_next(last, j):
        token_out(last).wait_send()
        token_out(j).start()

    def w_block(k, which):
        return wg.at[k, pl.ds(pl.multiple_of(which * rows, 64), rows), :]

    def w_copy(kind, k, incoming):
        sent = (r, r, r ^ 2)[kind]
        came = (r ^ 1, r ^ 2, r ^ 3)[kind]
        block = w_block(k, came if incoming else sent)
        return remote(block, block, w_s.at[kind], w_r.at[kind, k], other_xl if kind == 1 else other_core)

    for k in range(pairs):
        w_copy(1, k, False).start()
        w_copy(0, k, False).start()

    def take_in(j):
        token_in(j).wait_recv()
        token_y(j, 0, False).start()
        token_y(j, 1, False).start()

    def hand_on(j):
        token_y(j, 0, True).wait_recv()
        token_y(j, 2, False).start()
        token_y(j, 1, True).wait_recv()
        token_y(j, 3, False).start()

    def token_ready(j):
        token_y(j, 2, True).wait_recv()
        token_y(j, 3, True).wait_recv()

    def rs_copy(way, d, k):
        sign = 1 if way == 0 else -1
        src = part.at[k, plane(sign * d)]
        dst = ring.at[way, d - 1, k]
        if d == 4:
            src, dst = src.at[way], dst.at[way]
        return remote(src, dst, rs_s.at[way, d - 1], rs_r.at[way, d - 1, k], z_up if way == 0 else z_dn)

    def products(k, first, second):
        lhs = jnp.concatenate([tok[plane(first)], tok[plane(second)]], axis=0)
        out = dot(lhs, wg[k])
        return [[out[i * length : (i + 1) * length, a * HS : (a + 1) * HS] for a in range(2)] for i in range(2)]

    def weight_on(k):
        w_copy(1, k, True).wait_recv()
        w_copy(2, k, False).start()

    def far_step(k):
        w_copy(0, k, True).wait_recv()
        w_copy(2, k, True).wait_recv()
        far, own = products(k, 4, 0)
        for a in range(2):
            part[k, plane(4), a] = far[a]
            part[k, z, a] = own[a]
        for way in range(2):
            rs_copy(way, 4, k).start()

    token_next(2, 4)
    take_in(2)
    token_next(0, 1)
    take_in(0)
    hand_on(2)
    token_next(4, 6)
    weight_on(0)
    weight_on(1)
    own_tokens.wait()
    hand_on(0)
    token_next(1, 3)
    token_out(5).start()
    take_in(1)
    weight_on(2)
    token_ready(0)
    far_step(0)
    weight_on(3)
    far_step(1)
    hand_on(1)
    far_step(2)
    weight_on(4)
    far_step(3)
    token_ready(2)
    far_step(4)
    for load in loads[1:]:
        load.wait()

    def transpose_tokens(s):
        tok_t[:, pl.ds(pl.multiple_of(s * length, 128), length)] = tok[s].T

    def ring_step(d, k):
        both = products(k, d, -d)
        for way in range(2):
            t = plane(d if way == 0 else -d)
            rs_copy(way, d + 1, k).wait_recv()
            for a in range(2):
                if d == 3 and a != way:
                    part[k, t, a] = both[way][a]
                else:
                    part[k, t, a] = both[way][a] + ring[way, d, k, a]
            rs_copy(way, d, k).start()

    def pair_lanes(k):
        return pl.ds(pl.multiple_of(k * PW, 128), PW)

    def stacked_grads(k):
        grads = dctx_ref[:, pair_lanes(k)]
        return jnp.concatenate([grads[:, :HS], grads[:, HS:]], axis=0)

    token_ready(1)
    for k in range(pairs):
        ring_step(3, k)
        if k == 0:
            take_in(4)
        elif k == 1:
            take_in(6)
            hand_on(4)
        elif k == 2:
            hand_on(6)
            take_in(3)
        elif k == 3:
            take_in(5)
            hand_on(3)
        else:
            hand_on(5)
        wg_t[k * PW : (k + 1) * PW, :] = wg[k].T
    token_ready(3)
    token_ready(4)

    def second_step(k, carry):
        ring_step(2, k)
        transpose_tokens(plane(k + 2))
        return carry

    lax.fori_loop(0, pairs, second_step, 0)
    token_ready(5)
    token_ready(6)

    def third_step(k, carry):
        ring_step(1, k)
        d_probs_ref[k] = dot(stacked_grads(k), values_ref[...], ((1,), (1,)))

        @pl.when(k < 3)
        def _():
            transpose_tokens(plane(k - 1))

        return carry

    lax.fori_loop(0, pairs, third_step, 0)

    scale = 1.0 / HS**0.5
    row_id = lax.broadcasted_iota(jnp.int32, (2, length, length), 1)
    col_id = lax.broadcasted_iota(jnp.int32, (2, length, length), 2)
    causal = (col_id <= row_id).reshape(2 * length, length)
    dk_acc[...] = jnp.zeros_like(dk_acc)
    dv_acc[...] = jnp.zeros_like(dv_acc)

    def ag_copy(way, d, k, incoming):
        sign = -1 if way == 0 else 1
        block = dqall.at[k, plane(sign * (d if incoming else d - 1))]
        if d == 4:
            block = block.at[:, pl.ds(way * HS, HS)]
        return remote(block, block, ag_s.at[way, d - 1], ag_r.at[way, d - 1, k], z_up if way == 0 else z_dn)

    def attention_step(k, carry):
        for way in range(2):
            rs_copy(way, 1, k).wait_recv()
        keys = keys_ref[...]
        q = (part[k, z] + ring[0, 0, k] + ring[1, 0, k]).astype(BF16).reshape(2 * length, HS)
        d_probs = d_probs_ref[k]
        scores = jnp.where(causal, dot(q, keys, ((1,), (1,))) * scale, -1e30)
        e = jnp.exp(scores - jnp.max(scores, axis=-1, keepdims=True))
        probs = e * (1.0 / jnp.sum(e, axis=-1, keepdims=True))
        inner = jnp.sum(d_probs * probs, axis=-1, keepdims=True)
        ds = (probs * (d_probs - inner) * scale).astype(BF16)
        dq = dot(ds, keys).astype(BF16)
        dqall[k, z] = jnp.concatenate([dq[:length], dq[length:]], axis=1)
        for way in range(2):
            ag_copy(way, 1, k, False).start()
        low_ref[k], ds_ref[k], q_ref[k] = probs.astype(BF16), ds, q
        return carry

    lax.fori_loop(0, pairs, attention_step, 0)

    def attention_rest(k):
        low, ds, q = low_ref[k], ds_ref[k], q_ref[k]
        ctx = dot(low, values_ref[...]).astype(BF16)
        ctx_ref[:, pair_lanes(k)] = jnp.concatenate([ctx[:length], ctx[length:]], axis=1)
        dv_acc[...] += dot(low, stacked_grads(k), ((0,), (0,)))
        dk_acc[...] += dot(ds, q, ((0,), (0,)))

    groups = [(0, 1), (1, 2), (3, 2), (5, 2), (7, 1)]
    offsets = (0, -1, 1, -2, 2, -3, 3, 4)
    mid = cols // 2

    def y_copy(g, way, d):
        first, count = groups[g]
        slots = pl.ds(first, count)
        if d == 2:
            src = dts.at[slots, y2, :, pl.ds(way * mid, mid)]
            dst = yr2.at[way, slots]
        else:
            src = dts.at[slots, yp if way == 0 else ym]
            dst = yr1.at[way, slots]
        return remote(src, dst, y_s.at[way, d - 1], y_r.at[way, d - 1, g], y_up if way == 0 else y_dn)

    def d_token_block(g, n):
        first, count = groups[g]
        lhs = jnp.concatenate(
            [
                jnp.concatenate([dqall[k, plane(offsets[first + i])] for k in range(pairs)], axis=1)
                for i in range(count)
            ],
            axis=0,
        )
        lanes = pl.ds(pl.multiple_of(n * PW, 128), PW)
        out = dot(lhs, wg_t[:, lanes]).astype(BF16)
        for i in range(count):
            for owner in range(2 * NY):
                block = out[i * length + owner * 16 : i * length + (owner + 1) * 16]
                dts[first + i, owner % NY, (owner // NY) * 16 : (owner // NY + 1) * 16, lanes] = block

    def y_begin(g):
        for way in range(2):
            y_copy(g, way, 2).start()

    def y_first(g):
        first, count = groups[g]
        for way in range(2):
            y_copy(g, way, 2).wait_recv()
            to = yp if way == 0 else ym
            for i in range(count):
                own = dts[first + i, to, :, way * mid : (way + 1) * mid].astype(F32)
                came = yr2[way, first + i].astype(F32)
                dts[first + i, to, :, way * mid : (way + 1) * mid] = (own + came).astype(BF16)
            y_copy(g, way, 1).start()

    batches = [(0, 3), (3, 2), (5, 3)]

    def x_copy(b):
        first, count = batches[b]
        slots = pl.ds(first, count)
        return remote(red.at[slots, 1 - xh], xr.at[slots], x_s, x_r.at[b], other_xh)

    def y_second(g):
        first, count = groups[g]
        for way in range(2):
            y_copy(g, way, 1).wait_recv()
        for i in range(count):
            slot = first + i
            total = dts[slot, y].astype(F32) + yr1[0, slot].astype(F32) + yr1[1, slot].astype(F32)
            for side in range(2):
                red[slot, side] = total[side * 16 : (side + 1) * 16].astype(BF16)

    def home_copy(slot):
        block = dtk.at[:, pl.ds(pl.multiple_of(z * depth, 128), depth)]
        return remote(fin.at[slot], block, zd_s, zd_r.at[slot], at_z(plane(offsets[slot])))

    def home_in(slot):
        block = dtk.at[:, pl.ds(pl.multiple_of(plane(-offsets[slot]) * depth, 128), depth)]
        return remote(fin.at[slot], block, zd_s, zd_r.at[slot], z_up)

    def x_done(b):
        first, count = batches[b]
        x_copy(b).wait_recv()
        for i in range(count):
            slot = first + i
            total = (red[slot, xh].astype(F32) + xr[slot].astype(F32)).astype(BF16)
            if slot == 0:
                dtk[:, pl.ds(pl.multiple_of(z * depth, 128), depth)] = total
            else:
                fin[slot] = total
                home_copy(slot).start()

    def gc_copy(k):
        return remote(gs.at[k], gcr.at[k], gc_s, gc_r.at[k], other_core)

    def gx_copy(k):
        return remote(gxs.at[k], gxr.at[k], gx_s, gx_r.at[k], other_xl)

    def own_rows(side, core):
        return pl.ds(pl.multiple_of((side * 2 + core) * rows, 64), rows)

    def core_sum(k):
        gc_copy(k).wait_recv()
        away = 1 - xl
        gxs[k] = (ga[k, own_rows(away, c), :] + gcr[k, away].astype(F32)).astype(BF16)
        gx_copy(k).start()

    def grad_block(k):
        ga[k] = dot(tok_t[...], dqall[k].reshape(NZ * length, PW))
        for side in range(2):
            gs[k, side] = ga[k, own_rows(side, 1 - c), :].astype(BF16)
        gc_copy(k).start()

    def gather_step(d, k):
        for way in range(2):
            ag_copy(way, d, k, True).wait_recv()
            if d < 4:
                ag_copy(way, d + 1, k, False).start()

    def d_token_blocks(g, low, high):
        def step(n, carry):
            d_token_block(g, n)
            return carry

        lax.fori_loop(low, high, step, 0)

    def grad_done(k):
        gx_copy(k).wait_recv()
        mine = ga[k, own_rows(xl, c), :] + gcr[k, xl].astype(F32) + gxr[k].astype(F32)
        grad_ref[:, k * PW : (k + 1) * PW] = mine

    early = 2
    for step in range(4 * early):
        d, k = step // early + 1, step % early
        gather_step(d, k)
        if step < pairs:
            attention_rest(step)
            d_token_block(0, step)
        if step == pairs - 1:
            y_begin(0)
        if d == 4:
            grad_block(k)
    dk_ref[...] = dk_acc[...].astype(BF16)
    dv_ref[...] = dv_acc[...].astype(BF16)
    kept = ((ctx_ref, ctx_hbm), (dk_ref, dk_hbm), (dv_ref, dv_hbm))
    stores = [pltpu.make_async_copy(src, dst, out_sem.at[i]) for i, (src, dst) in enumerate(kept)]
    for store in stores:
        store.start()
    y_first(0)
    core_sum(0)
    gather_step(1, 2)
    core_sum(1)
    gather_step(1, 3)
    gather_step(1, 4)
    d_token_blocks(1, 0, pairs)
    y_begin(1)
    for k in range(early, pairs):
        gather_step(2, k)
    d_token_blocks(2, 0, pairs)
    y_begin(2)
    y_second(0)
    gather_step(3, 2)
    gather_step(3, 3)
    y_first(1)
    gather_step(3, 4)
    d_token_blocks(3, 0, pairs)
    y_begin(3)
    gather_step(4, 2)
    grad_block(2)
    y_first(2)
    gather_step(4, 3)
    grad_block(3)
    core_sum(2)
    gather_step(4, 4)
    d_token_blocks(4, 0, pairs)
    y_begin(4)
    y_second(1)
    x_copy(0).start()
    grad_block(4)
    core_sum(3)
    y_first(3)
    core_sum(4)
    y_first(4)
    y_second(2)
    x_copy(1).start()
    x_done(0)
    grad_done(0)
    grad_done(1)
    y_second(3)
    y_second(4)
    x_copy(2).start()
    grad_done(2)
    x_done(1)
    grad_done(3)
    x_done(2)
    grad_done(4)
    grad_store = pltpu.make_async_copy(grad_ref, grad_hbm, out_sem.at[3])
    grad_store.start()
    for slot in range(1, NZ):
        home_in(slot).wait_recv()
    dtok_store = pltpu.make_async_copy(dtk, dtok_hbm, out_sem.at[4])
    dtok_store.start()

    def sent(src, sem):
        remote(src, src, sem, gc_r.at[0], other_core).wait_send()

    for j in (3, 5, 6):
        token_out(j).wait_send()
    for kind in range(4):
        sent(tok.at[pl.ds(0, NZ - 1), pl.ds(0, half_rows if kind >= 2 else quarter), :], ty_s.at[kind])
    for kind in range(3):
        sent(wg.at[:, pl.ds(0, rows), :], w_s.at[kind])
    for way in range(2):
        for d in (1, 2, 3):
            sent(part.at[:, 0], rs_s.at[way, d - 1])
            sent(dqall.at[:, 0], ag_s.at[way, d - 1])
        sent(part.at[:, 0, 0], rs_s.at[way, 3])
        sent(dqall.at[:, 0, :, pl.ds(0, HS)], ag_s.at[way, 3])
        sent(dts.at[:, 0], y_s.at[way, 0])
        sent(dts.at[:, 0, :, pl.ds(0, mid)], y_s.at[way, 1])
    sent(fin.at[pl.ds(1, NZ - 1)], zd_s)
    sent(xr, x_s)
    sent(gs, gc_s)
    sent(gxs, gx_s)
    for store in stores + [grad_store, dtok_store]:
        store.wait()


def fused(tokens, master, keys, values, d_context):
    length, width = tokens.shape
    rows, cols = master.shape
    depth, pairs, mid, quarter = 4 * rows, cols // PW, cols // 2, length // NY
    vmem, dma = pltpu.VMEM, pltpu.SemaphoreType.DMA
    anywhere = pl.BlockSpec(memory_space=pl.ANY)
    return pl.pallas_call(
        kernel,
        out_shape=(
            jax.ShapeDtypeStruct((length, cols), BF16),
            jax.ShapeDtypeStruct((length, HS), BF16),
            jax.ShapeDtypeStruct((length, HS), BF16),
            jax.ShapeDtypeStruct((length // 8, width), BF16),
            jax.ShapeDtypeStruct((rows, cols), F32),
        ),
        in_specs=[anywhere] * 5,
        out_specs=[anywhere] * 5,
        scratch_shapes=[
            vmem((rows, cols), F32),
            vmem((length, HS), BF16),
            vmem((length, HS), BF16),
            vmem((length, cols), BF16),
            vmem((length, cols), BF16),
            vmem((length, HS), BF16),
            vmem((length, HS), BF16),
            vmem((rows, cols), F32),
            vmem((NZ, length, depth), BF16),
            vmem((depth, NZ * length), BF16),
            vmem((pairs, depth, PW), BF16),
            vmem((cols, depth), BF16),
            vmem((pairs, NZ, 2, length, HS), F32),
            vmem((2, 4, pairs, 2, length, HS), F32),
            vmem((pairs, NZ, length, PW), BF16),
            vmem((length, HS), F32),
            vmem((length, HS), F32),
            vmem((pairs, 2 * length, HS), F32),
            vmem((pairs, 2 * length, HS), BF16),
            vmem((pairs, 2 * length, HS), BF16),
            vmem((pairs, 2 * length, HS), BF16),
            vmem((NZ, NY, quarter, depth), BF16),
            vmem((2, NZ, quarter, mid), BF16),
            vmem((2, NZ, quarter, depth), BF16),
            vmem((NZ, 2, 16, depth), BF16),
            vmem((NZ, 16, depth), BF16),
            vmem((NZ, 16, depth), BF16),
            vmem((length // 8, width), BF16),
            vmem((pairs, depth, PW), F32),
            vmem((pairs, 2, rows, PW), BF16),
            vmem((pairs, 2, rows, PW), BF16),
            vmem((pairs, rows, PW), BF16),
            vmem((pairs, rows, PW), BF16),
            dma((4,)),
            dma((5,)),
            dma,
            dma((3,)), dma((3, pairs)),
            dma((NZ - 1,)), dma((NZ - 1,)),
            dma((4,)), dma((4, NZ - 1)),
            dma((2, 4)), dma((2, 4, pairs)),
            dma((2, 4)), dma((2, 4, pairs)),
            dma((2, 2)), dma((2, 2, 5)),
            dma, dma((3,)),
            dma, dma((NZ,)),
            dma, dma((pairs,)),
            dma, dma((pairs,)),
        ],
        compiler_params=pltpu.CompilerParams(
            collective_id=0, has_side_effects=True, vmem_limit_bytes=54 * 1024 * 1024
        ),
    )(tokens, master, keys, values, d_context)


def finish_kernel(*refs):
    wide, small, outs, tidy = refs[:4], refs[4:8], refs[8:11], refs[11:15]
    old, news, held, wide_in, new_out, small_in, small_out = refs[15], refs[16], refs[17:21], *refs[21:]
    parts, rows = old.shape[1], old.shape[2]
    came = [
        [pltpu.make_async_copy(wide[n].at[pl.ds(i * rows, rows)], old.at[n, i], wide_in.at[n, i]) for n in range(4)]
        for i in range(parts)
    ]
    first = [pltpu.make_async_copy(a, b, small_in.at[i]) for i, (a, b) in enumerate(zip(small, held))]
    second = [pltpu.make_async_copy(a, b, small_out.at[i]) for i, (a, b) in enumerate(zip(held, tidy))]
    for copy in came[0] + first + sum(came[1:], []):
        copy.start()
    writes = []
    for i in range(parts):
        for copy in came[i]:
            copy.wait()
        for n, value in enumerate(adam_piece(old[1, i], old[2, i], old[3, i], old[0, i])):
            news[n, i] = value
            writes.append(pltpu.make_async_copy(news.at[n, i], outs[n].at[pl.ds(i * rows, rows)], new_out.at[n, i]))
            writes[-1].start()
        if i == 0:
            for a, b in zip(first, second):
                a.wait()
                b.start()
    for copy in second + writes:
        copy.wait()


def finish(gradient, master, one, two, small):
    rows, cols = master.shape
    parts = 5
    anywhere = pl.BlockSpec(memory_space=pl.ANY)
    vmem, dma = pltpu.VMEM, pltpu.SemaphoreType.DMA
    like = jax.ShapeDtypeStruct((rows, cols), F32)
    return pl.pallas_call(
        finish_kernel,
        out_shape=[like] * 3 + [jax.ShapeDtypeStruct(a.shape, a.dtype) for a in small],
        in_specs=[anywhere] * 8,
        out_specs=[anywhere] * 7,
        scratch_shapes=[vmem((4, parts, rows // parts, cols), F32), vmem((3, parts, rows // parts, cols), F32)]
        + [vmem(a.shape, a.dtype) for a in small]
        + [dma((4, parts)), dma((3, parts)), dma((4,)), dma((4,))],
        compiler_params=pltpu.CompilerParams(vmem_limit_bytes=60 * 1024 * 1024),
    )(gradient, master, one, two, *small)


def body(tokens, master, moment_one, moment_two, keys, values, d_context):
    *small, gradient = fused(tokens, master, keys, values, d_context)
    new_master, new_one, new_two, *small = finish(gradient, master, moment_one, moment_two, small)
    return (*small, new_master, new_one, new_two)


def solution(mesh):
    both = P("node", "local")
    return jax.shard_map(
        body,
        mesh=mesh,
        in_specs=(P("node", None), both, both, both, both, both, both),
        out_specs=(both, both, both, P(("node", "local"), None), both, both, both),
        check_vma=False,
    )
```

```python
import functools

import jax
import jax.numpy as jnp
from jax import lax
from jax.experimental import pallas as pl
from jax.experimental.pallas import tpu as pltpu
from jax.sharding import PartitionSpec as P

MESH = pl.DeviceIdType.MESH
HS = 128
NZ, NY = 8, 4
PW = 2 * HS
ORDER = (4, 3, 5, 2, 6, 1, 7)
F32, BF16 = jnp.float32, jnp.bfloat16


def adam_piece(master, moment_one, moment_two, gradient):
    new_one = 0.9 * moment_one + 0.1 * gradient
    new_two = 0.999 * moment_two + 0.001 * gradient * gradient
    first_hat = new_one / (1.0 - 0.9**10)
    second_hat = new_two / (1.0 - 0.999**10)
    new_master = master - 0.001 * first_hat / (jnp.sqrt(second_hat) + 1e-08)
    return (new_master, new_one, new_two)


def dot(a, b, dims=((1,), (0,))):
    return lax.dot_general(a, b, (dims, ((), ())), preferred_element_type=F32)


def kernel(
    tokens_hbm, master_hbm, keys_hbm, values_hbm, dctx_hbm,
    ctx_hbm, dk_hbm, dv_hbm, dtok_hbm, grad_hbm,
    master_ref, keys_ref, values_ref, dctx_ref, ctx_ref, dk_ref, dv_ref, grad_ref,
    tok, tok_t, wg, wg_t, part, ring, dqall, dk_acc, dv_acc, d_probs_ref, low_ref, ds_ref, q_ref,
    dts, yr2, yr1, red, xr, fin, dtk,
    ga, gs, gcr, gxs, gxr,
    in_sem, out_sem, own_sem, w_s, w_r, tz_s, tz_r, ty_s, ty_r, rs_s, rs_r, ag_s, ag_r, y_s, y_r, x_s, x_r, zd_s, zd_r,
    gc_s, gc_r, gx_s, gx_r,
):
    length = keys_ref.shape[0]
    rows, cols = master_ref.shape
    depth = 4 * rows
    pairs = cols // PW
    node, local = lax.axis_index("node"), lax.axis_index("local")
    z, r = node // 4, node % 4
    xl, c = r // 2, r % 2
    xh, y = local // NY, local % NY
    quarter = length // NY
    half_rows = quarter // 2

    def plane(offset):
        return (z + offset + NZ) % NZ

    def at_z(where):
        return {"node": where * 4 + r, "local": local}

    def at_y(where):
        return {"node": node, "local": xh * NY + where}

    z_up, z_dn = at_z(plane(1)), at_z(plane(-1))
    yp, ym, y2 = (y + 1) % NY, (y + 3) % NY, (y + 2) % NY
    y_up, y_dn = at_y(yp), at_y(ym)
    other_core = {"node": z * 4 + xl * 2 + (1 - c), "local": local}
    other_xl = {"node": z * 4 + (1 - xl) * 2 + c, "local": local}
    other_xh = {"node": node, "local": (1 - xh) * NY + y}

    def remote(src, dst, send_sem, recv_sem, device):
        return pltpu.make_async_remote_copy(
            src_ref=src, dst_ref=dst, send_sem=send_sem, recv_sem=recv_sem,
            device_id=device, device_id_type=MESH,
        )

    barrier = pltpu.get_barrier_semaphore()
    partners = [at_z(plane(d)) for d in range(1, NZ)] + [y_up, y_dn, other_core, other_xl, other_xh]
    for device in partners:
        pl.semaphore_signal(barrier, inc=1, device_id=device, device_id_type=MESH)
    held = ((master_hbm, master_ref), (keys_hbm, keys_ref), (values_hbm, values_ref), (dctx_hbm, dctx_ref))
    loads = [pltpu.make_async_copy(src, dst, in_sem.at[i]) for i, (src, dst) in enumerate(held)]
    for load in loads:
        load.start()
    own_tokens = pltpu.make_async_copy(
        tokens_hbm.at[:, pl.ds(pl.multiple_of(z * depth, 128), depth)], tok.at[z], own_sem
    )
    own_tokens.start()
    loads[0].wait()
    for k in range(pairs):
        wg[k, pl.ds(pl.multiple_of(r * rows, 64), rows), :] = master_ref[:, k * PW : (k + 1) * PW].astype(BF16)
    pl.semaphore_wait(barrier, len(partners))

    def row_block(base, count):
        return pl.ds(pl.multiple_of(base, 16), count)

    def token_out(j):
        to = plane(ORDER[j])
        src = tokens_hbm.at[row_block(y * quarter, quarter), pl.ds(pl.multiple_of(to * depth, 128), depth)]
        return remote(src, tok.at[z, row_block(y * quarter, quarter), :], tz_s.at[j], tz_r.at[j], at_z(to))

    def token_in(j):
        block = tok.at[plane(-ORDER[j]), row_block(y * quarter, quarter), :]
        return remote(block, block, tz_s.at[j], tz_r.at[j], z_up)

    def token_y(j, kind, incoming):
        s = plane(-ORDER[j])
        me = (yp if kind in (1, 3) else ym) if incoming else y
        base, count = me * quarter, quarter
        if kind >= 2:
            origin = y2 if incoming else (ym if kind == 2 else yp)
            base, count = origin * quarter + (0 if kind == 2 else half_rows), half_rows
        block = tok.at[s, row_block(base, count), :]
        return remote(block, block, ty_s.at[kind], ty_r.at[kind, j], y_up if kind in (0, 2) else y_dn)

    token_out(0).start()
    token_out(2).start()

    def token_next(last, j):
        token_out(last).wait_send()
        token_out(j).start()

    def w_block(k, which):
        return wg.at[k, pl.ds(pl.multiple_of(which * rows, 64), rows), :]

    def w_copy(kind, k, incoming):
        sent = (r, r, r ^ 2)[kind]
        came = (r ^ 1, r ^ 2, r ^ 3)[kind]
        block = w_block(k, came if incoming else sent)
        return remote(block, block, w_s.at[kind], w_r.at[kind, k], other_xl if kind == 1 else other_core)

    for k in range(pairs):
        w_copy(1, k, False).start()
        w_copy(0, k, False).start()

    def take_in(j):
        token_in(j).wait_recv()
        token_y(j, 0, False).start()
        token_y(j, 1, False).start()

    def hand_on(j):
        token_y(j, 0, True).wait_recv()
        token_y(j, 2, False).start()
        token_y(j, 1, True).wait_recv()
        token_y(j, 3, False).start()

    def token_ready(j):
        token_y(j, 2, True).wait_recv()
        token_y(j, 3, True).wait_recv()

    def rs_copy(way, d, k):
        sign = 1 if way == 0 else -1
        src = part.at[k, plane(sign * d)]
        dst = ring.at[way, d - 1, k]
        if d == 4:
            src, dst = src.at[way], dst.at[way]
        return remote(src, dst, rs_s.at[way, d - 1], rs_r.at[way, d - 1, k], z_up if way == 0 else z_dn)

    def products(k, first, second):
        lhs = jnp.concatenate([tok[plane(first)], tok[plane(second)]], axis=0)
        out = dot(lhs, wg[k])
        return [[out[i * length : (i + 1) * length, a * HS : (a + 1) * HS] for a in range(2)] for i in range(2)]

    def weight_on(k):
        w_copy(1, k, True).wait_recv()
        w_copy(2, k, False).start()

    def far_step(k):
        w_copy(0, k, True).wait_recv()
        w_copy(2, k, True).wait_recv()
        far, own = products(k, 4, 0)
        for a in range(2):
            part[k, plane(4), a] = far[a]
            part[k, z, a] = own[a]
        for way in range(2):
            rs_copy(way, 4, k).start()

    def transpose_weight(k):
        wg_t[pl.ds(pl.multiple_of(k * PW, PW), PW), :] = wg[k].T

    token_next(2, 4)
    take_in(2)
    token_next(0, 1)
    take_in(0)
    hand_on(2)
    token_next(4, 6)
    weight_on(0)
    weight_on(1)
    own_tokens.wait()
    hand_on(0)
    token_next(1, 3)
    token_out(5).start()
    take_in(1)
    weight_on(2)
    token_ready(0)
    far_step(0)
    weight_on(3)
    far_step(1)
    hand_on(1)
    transpose_weight(0)
    far_step(2)
    weight_on(4)
    far_step(3)
    token_ready(2)
    far_step(4)
    transpose_weight(1)
    for load in loads[1:]:
        load.wait()

    def transpose_tokens(s):
        tok_t[:, pl.ds(pl.multiple_of(s * length, 128), length)] = tok[s].T

    def ring_step(d, k):
        both = products(k, d, -d)
        for way in range(2):
            t = plane(d if way == 0 else -d)
            rs_copy(way, d + 1, k).wait_recv()
            for a in range(2):
                if d == 3 and a != way:
                    part[k, t, a] = both[way][a]
                else:
                    part[k, t, a] = both[way][a] + ring[way, d, k, a]
            rs_copy(way, d, k).start()

    def pair_lanes(k):
        return pl.ds(pl.multiple_of(k * PW, 128), PW)

    def stacked_grads(k):
        grads = dctx_ref[:, pair_lanes(k)]
        return jnp.concatenate([grads[:, :HS], grads[:, HS:]], axis=0)

    token_ready(1)
    for k in range(pairs):
        ring_step(3, k)
        if k == 0:
            take_in(4)
        elif k == 1:
            take_in(6)
            hand_on(4)
        elif k == 2:
            hand_on(6)
            take_in(3)
        elif k == 3:
            take_in(5)
            hand_on(3)
        else:
            hand_on(5)
    token_ready(3)
    token_ready(4)

    def second_step(k, carry):
        ring_step(2, k)
        transpose_tokens(plane(k + 2))
        return carry

    lax.fori_loop(0, pairs, second_step, 0)
    token_ready(5)
    token_ready(6)

    def third_step(k, carry):
        ring_step(1, k)
        d_probs_ref[k] = dot(stacked_grads(k), values_ref[...], ((1,), (1,)))

        @pl.when(k < 3)
        def _():
            transpose_weight(k + 2)

        @pl.when(k >= 2)
        def _():
            transpose_tokens(plane(k - 3))

        return carry

    lax.fori_loop(0, pairs, third_step, 0)

    scale = 1.0 / HS**0.5
    row_id = lax.broadcasted_iota(jnp.int32, (2, length, length), 1)
    col_id = lax.broadcasted_iota(jnp.int32, (2, length, length), 2)
    causal = (col_id <= row_id).reshape(2 * length, length)
    dk_acc[...] = jnp.zeros_like(dk_acc)
    dv_acc[...] = jnp.zeros_like(dv_acc)

    def ag_copy(way, d, k, incoming):
        sign = -1 if way == 0 else 1
        block = dqall.at[k, plane(sign * (d if incoming else d - 1))]
        if d == 4:
            block = block.at[:, pl.ds(way * HS, HS)]
        return remote(block, block, ag_s.at[way, d - 1], ag_r.at[way, d - 1, k], z_up if way == 0 else z_dn)

    def attention_step(k, carry):
        for way in range(2):
            rs_copy(way, 1, k).wait_recv()
        keys = keys_ref[...]
        q = (part[k, z] + ring[0, 0, k] + ring[1, 0, k]).astype(BF16).reshape(2 * length, HS)
        d_probs = d_probs_ref[k]
        scores = jnp.where(causal, dot(q, keys, ((1,), (1,))) * scale, -1e30)
        e = jnp.exp(scores - jnp.max(scores, axis=-1, keepdims=True))
        probs = e * (1.0 / jnp.sum(e, axis=-1, keepdims=True))
        inner = jnp.sum(d_probs * probs, axis=-1, keepdims=True)
        ds = (probs * (d_probs - inner) * scale).astype(BF16)
        dq = dot(ds, keys).astype(BF16)
        dqall[k, z] = jnp.concatenate([dq[:length], dq[length:]], axis=1)
        for way in range(2):
            ag_copy(way, 1, k, False).start()
        low_ref[k], ds_ref[k], q_ref[k] = probs.astype(BF16), ds, q
        return carry

    lax.fori_loop(0, pairs, attention_step, 0)

    def attention_rest(k):
        low, ds, q = low_ref[k], ds_ref[k], q_ref[k]
        ctx = dot(low, values_ref[...]).astype(BF16)
        ctx_ref[:, pair_lanes(k)] = jnp.concatenate([ctx[:length], ctx[length:]], axis=1)
        dv_acc[...] += dot(low, stacked_grads(k), ((0,), (0,)))
        dk_acc[...] += dot(ds, q, ((0,), (0,)))

    groups = [(0, 1), (1, 2), (3, 2), (5, 2), (7, 1)]
    offsets = (0, -1, 1, -2, 2, -3, 3, 4)
    mid = cols // 2

    def y_copy(g, way, d):
        first, count = groups[g]
        slots = pl.ds(first, count)
        if d == 2:
            src = dts.at[slots, y2, :, pl.ds(way * mid, mid)]
            dst = yr2.at[way, slots]
        else:
            src = dts.at[slots, yp if way == 0 else ym]
            dst = yr1.at[way, slots]
        return remote(src, dst, y_s.at[way, d - 1], y_r.at[way, d - 1, g], y_up if way == 0 else y_dn)

    def d_token_block(g, n):
        first, count = groups[g]
        lhs = jnp.concatenate(
            [
                jnp.concatenate([dqall[k, plane(offsets[first + i])] for k in range(pairs)], axis=1)
                for i in range(count)
            ],
            axis=0,
        )
        lanes = pl.ds(pl.multiple_of(n * PW, 128), PW)
        out = dot(lhs, wg_t[:, lanes]).astype(BF16)
        for i in range(count):
            for owner in range(2 * NY):
                block = out[i * length + owner * 16 : i * length + (owner + 1) * 16]
                dts[first + i, owner % NY, (owner // NY) * 16 : (owner // NY + 1) * 16, lanes] = block

    def y_begin(g):
        for way in range(2):
            y_copy(g, way, 2).start()

    def y_first(g):
        first, count = groups[g]
        for way in range(2):
            y_copy(g, way, 2).wait_recv()
            to = yp if way == 0 else ym
            for i in range(count):
                own = dts[first + i, to, :, way * mid : (way + 1) * mid].astype(F32)
                came = yr2[way, first + i].astype(F32)
                dts[first + i, to, :, way * mid : (way + 1) * mid] = (own + came).astype(BF16)
            y_copy(g, way, 1).start()

    batches = [(0, 3), (3, 2), (5, 3)]

    def x_copy(b):
        first, count = batches[b]
        slots = pl.ds(first, count)
        return remote(red.at[slots, 1 - xh], xr.at[slots], x_s, x_r.at[b], other_xh)

    def y_second(g):
        first, count = groups[g]
        for way in range(2):
            y_copy(g, way, 1).wait_recv()
        for i in range(count):
            slot = first + i
            total = dts[slot, y].astype(F32) + yr1[0, slot].astype(F32) + yr1[1, slot].astype(F32)
            for side in range(2):
                red[slot, side] = total[side * 16 : (side + 1) * 16].astype(BF16)

    def home_copy(slot):
        block = dtk.at[:, pl.ds(pl.multiple_of(z * depth, 128), depth)]
        return remote(fin.at[slot], block, zd_s, zd_r.at[slot], at_z(plane(offsets[slot])))

    def home_in(slot):
        block = dtk.at[:, pl.ds(pl.multiple_of(plane(-offsets[slot]) * depth, 128), depth)]
        return remote(fin.at[slot], block, zd_s, zd_r.at[slot], z_up)

    def x_done(b):
        first, count = batches[b]
        x_copy(b).wait_recv()
        for i in range(count):
            slot = first + i
            total = (red[slot, xh].astype(F32) + xr[slot].astype(F32)).astype(BF16)
            if slot == 0:
                dtk[:, pl.ds(pl.multiple_of(z * depth, 128), depth)] = total
            else:
                fin[slot] = total
                home_copy(slot).start()

    def gc_copy(k):
        return remote(gs.at[k], gcr.at[k], gc_s, gc_r.at[k], other_core)

    def gx_copy(k):
        return remote(gxs.at[k], gxr.at[k], gx_s, gx_r.at[k], other_xl)

    def own_rows(side, core):
        return pl.ds(pl.multiple_of((side * 2 + core) * rows, 64), rows)

    def core_sum(k):
        gc_copy(k).wait_recv()
        away = 1 - xl
        gxs[k] = (ga[k, own_rows(away, c), :] + gcr[k, away].astype(F32)).astype(BF16)
        gx_copy(k).start()

    def grad_block(k):
        ga[k] = dot(tok_t[...], dqall[k].reshape(NZ * length, PW))
        for side in range(2):
            gs[k, side] = ga[k, own_rows(side, 1 - c), :].astype(BF16)
        gc_copy(k).start()

    def gather_step(d, k):
        for way in range(2):
            ag_copy(way, d, k, True).wait_recv()
            if d < 4:
                ag_copy(way, d + 1, k, False).start()

    def d_token_blocks(g, low, high):
        def step(n, carry):
            d_token_block(g, n)
            return carry

        lax.fori_loop(low, high, step, 0)

    def grad_done(k):
        gx_copy(k).wait_recv()
        mine = ga[k, own_rows(xl, c), :] + gcr[k, xl].astype(F32) + gxr[k].astype(F32)
        grad_ref[:, k * PW : (k + 1) * PW] = mine

    for k in range(pairs):
        gather_step(1, k)
        d_token_block(0, k)
        if k < 2:
            attention_rest(k)
    y_begin(0)
    d_token_blocks(1, 0, pairs)
    y_begin(1)
    gather_step(2, 0)
    attention_rest(2)
    gather_step(2, 1)
    attention_rest(3)
    gather_step(2, 2)
    attention_rest(4)
    dk_ref[...] = dk_acc[...].astype(BF16)
    dv_ref[...] = dv_acc[...].astype(BF16)
    kept = ((ctx_ref, ctx_hbm), (dk_ref, dk_hbm), (dv_ref, dv_hbm))
    stores = [pltpu.make_async_copy(src, dst, out_sem.at[i]) for i, (src, dst) in enumerate(kept)]
    for store in stores:
        store.start()
    y_first(0)
    gather_step(3, 0)
    gather_step(2, 3)
    gather_step(3, 1)
    gather_step(2, 4)
    d_token_blocks(2, 0, pairs)
    y_begin(2)
    y_first(1)
    gather_step(3, 2)
    gather_step(4, 0)
    grad_block(0)
    y_second(0)
    gather_step(3, 3)
    gather_step(4, 1)
    grad_block(1)
    core_sum(0)
    gather_step(3, 4)
    d_token_blocks(3, 0, pairs)
    y_begin(3)
    y_first(2)
    y_second(1)
    x_copy(0).start()
    gather_step(4, 2)
    grad_block(2)
    core_sum(1)
    gather_step(4, 3)
    grad_block(3)
    core_sum(2)
    gather_step(4, 4)
    d_token_blocks(4, 0, pairs)
    y_begin(4)
    y_second(2)
    x_copy(1).start()
    grad_block(4)
    core_sum(3)
    y_first(3)
    core_sum(4)
    y_first(4)
    x_done(0)
    grad_done(0)
    y_second(3)
    grad_done(1)
    y_second(4)
    x_copy(2).start()
    x_done(1)
    grad_done(2)
    grad_done(3)
    x_done(2)
    grad_done(4)
    grad_store = pltpu.make_async_copy(grad_ref, grad_hbm, out_sem.at[3])
    grad_store.start()
    for slot in range(1, NZ):
        home_in(slot).wait_recv()
    dtok_store = pltpu.make_async_copy(dtk, dtok_hbm, out_sem.at[4])
    dtok_store.start()

    def sent(src, sem):
        remote(src, src, sem, gc_r.at[0], other_core).wait_send()

    for j in (3, 5, 6):
        token_out(j).wait_send()
    for kind in range(4):
        sent(tok.at[pl.ds(0, NZ - 1), pl.ds(0, half_rows if kind >= 2 else quarter), :], ty_s.at[kind])
    for kind in range(3):
        sent(wg.at[:, pl.ds(0, rows), :], w_s.at[kind])
    for way in range(2):
        for d in (1, 2, 3):
            sent(part.at[:, 0], rs_s.at[way, d - 1])
            sent(dqall.at[:, 0], ag_s.at[way, d - 1])
        sent(part.at[:, 0, 0], rs_s.at[way, 3])
        sent(dqall.at[:, 0, :, pl.ds(0, HS)], ag_s.at[way, 3])
        sent(dts.at[:, 0], y_s.at[way, 0])
        sent(dts.at[:, 0, :, pl.ds(0, mid)], y_s.at[way, 1])
    sent(fin.at[pl.ds(1, NZ - 1)], zd_s)
    sent(xr, x_s)
    sent(gs, gc_s)
    sent(gxs, gx_s)
    for store in stores + [grad_store, dtok_store]:
        store.wait()


def fused(tokens, master, keys, values, d_context):
    length, width = tokens.shape
    rows, cols = master.shape
    depth, pairs, mid, quarter = 4 * rows, cols // PW, cols // 2, length // NY
    vmem, dma = pltpu.VMEM, pltpu.SemaphoreType.DMA
    anywhere = pl.BlockSpec(memory_space=pl.ANY)
    return pl.pallas_call(
        kernel,
        out_shape=(
            jax.ShapeDtypeStruct((length, cols), BF16),
            jax.ShapeDtypeStruct((length, HS), BF16),
            jax.ShapeDtypeStruct((length, HS), BF16),
            jax.ShapeDtypeStruct((length // 8, width), BF16),
            jax.ShapeDtypeStruct((rows, cols), F32),
        ),
        in_specs=[anywhere] * 5,
        out_specs=[anywhere] * 5,
        scratch_shapes=[
            vmem((rows, cols), F32),
            vmem((length, HS), BF16),
            vmem((length, HS), BF16),
            vmem((length, cols), BF16),
            vmem((length, cols), BF16),
            vmem((length, HS), BF16),
            vmem((length, HS), BF16),
            vmem((rows, cols), F32),
            vmem((NZ, length, depth), BF16),
            vmem((depth, NZ * length), BF16),
            vmem((pairs, depth, PW), BF16),
            vmem((cols, depth), BF16),
            vmem((pairs, NZ, 2, length, HS), F32),
            vmem((2, 4, pairs, 2, length, HS), F32),
            vmem((pairs, NZ, length, PW), BF16),
            vmem((length, HS), F32),
            vmem((length, HS), F32),
            vmem((pairs, 2 * length, HS), F32),
            vmem((pairs, 2 * length, HS), BF16),
            vmem((pairs, 2 * length, HS), BF16),
            vmem((pairs, 2 * length, HS), BF16),
            vmem((NZ, NY, quarter, depth), BF16),
            vmem((2, NZ, quarter, mid), BF16),
            vmem((2, NZ, quarter, depth), BF16),
            vmem((NZ, 2, 16, depth), BF16),
            vmem((NZ, 16, depth), BF16),
            vmem((NZ, 16, depth), BF16),
            vmem((length // 8, width), BF16),
            vmem((pairs, depth, PW), F32),
            vmem((pairs, 2, rows, PW), BF16),
            vmem((pairs, 2, rows, PW), BF16),
            vmem((pairs, rows, PW), BF16),
            vmem((pairs, rows, PW), BF16),
            dma((4,)),
            dma((5,)),
            dma,
            dma((3,)), dma((3, pairs)),
            dma((NZ - 1,)), dma((NZ - 1,)),
            dma((4,)), dma((4, NZ - 1)),
            dma((2, 4)), dma((2, 4, pairs)),
            dma((2, 4)), dma((2, 4, pairs)),
            dma((2, 2)), dma((2, 2, 5)),
            dma, dma((3,)),
            dma, dma((NZ,)),
            dma, dma((pairs,)),
            dma, dma((pairs,)),
        ],
        compiler_params=pltpu.CompilerParams(
            collective_id=0, has_side_effects=True, vmem_limit_bytes=54 * 1024 * 1024
        ),
    )(tokens, master, keys, values, d_context)


def finish_kernel(*refs):
    wide, small, outs, tidy = refs[:4], refs[4:8], refs[8:11], refs[11:15]
    old, news, held, wide_in, new_out, small_in, small_out = refs[15], refs[16], refs[17:21], *refs[21:]
    parts, rows = old.shape[1], old.shape[2]
    came = [
        [pltpu.make_async_copy(wide[n].at[pl.ds(i * rows, rows)], old.at[n, i], wide_in.at[n, i]) for n in range(4)]
        for i in range(parts)
    ]
    first = [pltpu.make_async_copy(a, b, small_in.at[i]) for i, (a, b) in enumerate(zip(small, held))]
    second = [pltpu.make_async_copy(a, b, small_out.at[i]) for i, (a, b) in enumerate(zip(held, tidy))]
    for copy in came[0] + first + sum(came[1:], []):
        copy.start()
    writes = []
    for i in range(parts):
        for copy in came[i]:
            copy.wait()
        for n, value in enumerate(adam_piece(old[1, i], old[2, i], old[3, i], old[0, i])):
            news[n, i] = value
            writes.append(pltpu.make_async_copy(news.at[n, i], outs[n].at[pl.ds(i * rows, rows)], new_out.at[n, i]))
            writes[-1].start()
        if i == 0:
            for a, b in zip(first, second):
                a.wait()
                b.start()
    for copy in second + writes:
        copy.wait()


def finish(gradient, master, one, two, small):
    rows, cols = master.shape
    parts = 5
    anywhere = pl.BlockSpec(memory_space=pl.ANY)
    vmem, dma = pltpu.VMEM, pltpu.SemaphoreType.DMA
    like = jax.ShapeDtypeStruct((rows, cols), F32)
    return pl.pallas_call(
        finish_kernel,
        out_shape=[like] * 3 + [jax.ShapeDtypeStruct(a.shape, a.dtype) for a in small],
        in_specs=[anywhere] * 8,
        out_specs=[anywhere] * 7,
        scratch_shapes=[vmem((4, parts, rows // parts, cols), F32), vmem((3, parts, rows // parts, cols), F32)]
        + [vmem(a.shape, a.dtype) for a in small]
        + [dma((4, parts)), dma((3, parts)), dma((4,)), dma((4,))],
        compiler_params=pltpu.CompilerParams(vmem_limit_bytes=60 * 1024 * 1024),
    )(gradient, master, one, two, *small)


def body(tokens, master, moment_one, moment_two, keys, values, d_context):
    *small, gradient = fused(tokens, master, keys, values, d_context)
    new_master, new_one, new_two, *small = finish(gradient, master, moment_one, moment_two, small)
    return (*small, new_master, new_one, new_two)


def solution(mesh):
    both = P("node", "local")
    return jax.shard_map(
        body,
        mesh=mesh,
        in_specs=(P("node", None), both, both, both, both, both, both),
        out_specs=(both, both, both, P(("node", "local"), None), both, both, both),
        check_vma=False,
    )
```

```python
import functools

import jax
import jax.numpy as jnp
from jax import lax
from jax.experimental import pallas as pl
from jax.experimental.pallas import tpu as pltpu
from jax.sharding import PartitionSpec as P

MESH = pl.DeviceIdType.MESH
HS = 128
NZ, NY = 8, 4
PW = 2 * HS
ORDER = (4, 3, 5, 2, 6, 1, 7)
F32, BF16 = jnp.float32, jnp.bfloat16


def adam_piece(master, moment_one, moment_two, gradient):
    new_one = 0.9 * moment_one + 0.1 * gradient
    new_two = 0.999 * moment_two + 0.001 * gradient * gradient
    first_hat = new_one / (1.0 - 0.9**10)
    second_hat = new_two / (1.0 - 0.999**10)
    new_master = master - 0.001 * first_hat / (jnp.sqrt(second_hat) + 1e-08)
    return (new_master, new_one, new_two)


def dot(a, b, dims=((1,), (0,))):
    return lax.dot_general(a, b, (dims, ((), ())), preferred_element_type=F32)


def kernel(
    tokens_hbm, master_hbm, keys_hbm, values_hbm, dctx_hbm,
    ctx_hbm, dk_hbm, dv_hbm, dtok_hbm, grad_hbm,
    master_ref, keys_ref, values_ref, dctx_ref, ctx_ref, dk_ref, dv_ref, grad_ref,
    tok, tok_t, wg, wg_t, part, ring, dqall, dk_acc, dv_acc, d_probs_ref, low_ref, ds_ref, q_ref,
    dts, yr2, yr1, red, xr, fin, dtk,
    ga, gs, gcr, gxs, gxr,
    in_sem, out_sem, own_sem, w_s, w_r, tz_s, tz_r, ty_s, ty_r, rs_s, rs_r, ag_s, ag_r, y_s, y_r, x_s, x_r, zd_s, zd_r,
    gc_s, gc_r, gx_s, gx_r,
):
    length = keys_ref.shape[0]
    rows, cols = master_ref.shape
    depth = 4 * rows
    pairs = cols // PW
    node, local = lax.axis_index("node"), lax.axis_index("local")
    z, r = node // 4, node % 4
    xl, c = r // 2, r % 2
    xh, y = local // NY, local % NY
    quarter = length // NY
    half_rows = quarter // 2

    def plane(offset):
        return (z + offset + NZ) % NZ

    def at_z(where):
        return {"node": where * 4 + r, "local": local}

    def at_y(where):
        return {"node": node, "local": xh * NY + where}

    z_up, z_dn = at_z(plane(1)), at_z(plane(-1))
    yp, ym, y2 = (y + 1) % NY, (y + 3) % NY, (y + 2) % NY
    y_up, y_dn = at_y(yp), at_y(ym)
    other_core = {"node": z * 4 + xl * 2 + (1 - c), "local": local}
    other_xl = {"node": z * 4 + (1 - xl) * 2 + c, "local": local}
    other_xh = {"node": node, "local": (1 - xh) * NY + y}

    def remote(src, dst, send_sem, recv_sem, device):
        return pltpu.make_async_remote_copy(
            src_ref=src, dst_ref=dst, send_sem=send_sem, recv_sem=recv_sem,
            device_id=device, device_id_type=MESH,
        )

    barrier = pltpu.get_barrier_semaphore()
    partners = [at_z(plane(d)) for d in range(1, NZ)] + [y_up, y_dn, other_core, other_xl, other_xh]
    for device in partners:
        pl.semaphore_signal(barrier, inc=1, device_id=device, device_id_type=MESH)
    held = ((master_hbm, master_ref), (keys_hbm, keys_ref), (values_hbm, values_ref), (dctx_hbm, dctx_ref))
    loads = [pltpu.make_async_copy(src, dst, in_sem.at[i]) for i, (src, dst) in enumerate(held)]
    for load in loads:
        load.start()
    own_tokens = pltpu.make_async_copy(
        tokens_hbm.at[:, pl.ds(pl.multiple_of(z * depth, 128), depth)], tok.at[z], own_sem
    )
    own_tokens.start()
    loads[0].wait()
    for k in range(pairs):
        wg[k, pl.ds(pl.multiple_of(r * rows, 64), rows), :] = master_ref[:, k * PW : (k + 1) * PW].astype(BF16)
    pl.semaphore_wait(barrier, len(partners))

    def row_block(base, count):
        return pl.ds(pl.multiple_of(base, 16), count)

    def token_out(j):
        to = plane(ORDER[j])
        src = tokens_hbm.at[row_block(y * quarter, quarter), pl.ds(pl.multiple_of(to * depth, 128), depth)]
        return remote(src, tok.at[z, row_block(y * quarter, quarter), :], tz_s.at[j], tz_r.at[j], at_z(to))

    def token_in(j):
        block = tok.at[plane(-ORDER[j]), row_block(y * quarter, quarter), :]
        return remote(block, block, tz_s.at[j], tz_r.at[j], z_up)

    def token_y(j, kind, incoming):
        s = plane(-ORDER[j])
        me = (yp if kind in (1, 3) else ym) if incoming else y
        base, count = me * quarter, quarter
        if kind >= 2:
            origin = y2 if incoming else (ym if kind == 2 else yp)
            base, count = origin * quarter + (0 if kind == 2 else half_rows), half_rows
        block = tok.at[s, row_block(base, count), :]
        return remote(block, block, ty_s.at[kind], ty_r.at[kind, j], y_up if kind in (0, 2) else y_dn)

    token_out(0).start()
    token_out(2).start()

    def token_next(last, j):
        token_out(last).wait_send()
        token_out(j).start()

    def w_block(k, which):
        return wg.at[k, pl.ds(pl.multiple_of(which * rows, 64), rows), :]

    def w_copy(kind, k, incoming):
        sent = (r, r, r ^ 2)[kind]
        came = (r ^ 1, r ^ 2, r ^ 3)[kind]
        block = w_block(k, came if incoming else sent)
        return remote(block, block, w_s.at[kind], w_r.at[kind, k], other_xl if kind == 1 else other_core)

    for k in range(pairs):
        w_copy(1, k, False).start()
        w_copy(0, k, False).start()

    def take_in(j):
        token_in(j).wait_recv()
        token_y(j, 0, False).start()
        token_y(j, 1, False).start()

    def hand_on(j):
        token_y(j, 0, True).wait_recv()
        token_y(j, 2, False).start()
        token_y(j, 1, True).wait_recv()
        token_y(j, 3, False).start()

    def token_ready(j):
        token_y(j, 2, True).wait_recv()
        token_y(j, 3, True).wait_recv()

    def rs_copy(way, d, k):
        sign = 1 if way == 0 else -1
        src = part.at[k, plane(sign * d)]
        dst = ring.at[way, d - 1, k]
        if d == 4:
            src, dst = src.at[way], dst.at[way]
        return remote(src, dst, rs_s.at[way, d - 1], rs_r.at[way, d - 1, k], z_up if way == 0 else z_dn)

    def products(k, first, second):
        lhs = jnp.concatenate([tok[plane(first)], tok[plane(second)]], axis=0)
        out = dot(lhs, wg[k])
        return [[out[i * length : (i + 1) * length, a * HS : (a + 1) * HS] for a in range(2)] for i in range(2)]

    def weight_on(k):
        w_copy(1, k, True).wait_recv()
        w_copy(2, k, False).start()

    def far_step(k):
        w_copy(0, k, True).wait_recv()
        w_copy(2, k, True).wait_recv()
        far, own = products(k, 4, 0)
        for a in range(2):
            part[k, plane(4), a] = far[a]
            part[k, z, a] = own[a]
        for way in range(2):
            rs_copy(way, 4, k).start()

    def transpose_weight(k):
        wg_t[pl.ds(pl.multiple_of(k * PW, PW), PW), :] = wg[k].T

    token_next(2, 4)
    take_in(2)
    token_next(0, 1)
    take_in(0)
    hand_on(2)
    token_next(4, 6)
    weight_on(0)
    weight_on(1)
    own_tokens.wait()
    hand_on(0)
    token_next(1, 3)
    token_out(5).start()
    take_in(1)
    weight_on(2)
    token_ready(0)
    far_step(0)
    weight_on(3)
    far_step(1)
    hand_on(1)
    transpose_weight(0)
    far_step(2)
    weight_on(4)
    far_step(3)
    token_ready(2)
    far_step(4)
    transpose_weight(1)
    for load in loads[1:]:
        load.wait()

    def transpose_tokens(s):
        tok_t[:, pl.ds(pl.multiple_of(s * length, 128), length)] = tok[s].T

    def ring_step(d, k):
        both = products(k, d, -d)
        for way in range(2):
            t = plane(d if way == 0 else -d)
            rs_copy(way, d + 1, k).wait_recv()
            for a in range(2):
                if d == 3 and a != way:
                    part[k, t, a] = both[way][a]
                else:
                    part[k, t, a] = both[way][a] + ring[way, d, k, a]
            rs_copy(way, d, k).start()

    def pair_lanes(k):
        return pl.ds(pl.multiple_of(k * PW, 128), PW)

    def stacked_grads(k):
        grads = dctx_ref[:, pair_lanes(k)]
        return jnp.concatenate([grads[:, :HS], grads[:, HS:]], axis=0)

    token_ready(1)
    for k in range(pairs):
        ring_step(3, k)
        if k == 0:
            take_in(4)
        elif k == 1:
            take_in(6)
            hand_on(4)
        elif k == 2:
            hand_on(6)
            take_in(3)
        elif k == 3:
            take_in(5)
            hand_on(3)
        else:
            hand_on(5)
    token_ready(3)
    token_ready(4)

    def second_step(k, carry):
        ring_step(2, k)
        transpose_tokens(plane(k + 2))
        return carry

    lax.fori_loop(0, pairs, second_step, 0)
    token_ready(5)
    token_ready(6)

    def third_step(k, carry):
        ring_step(1, k)
        d_probs_ref[k] = dot(stacked_grads(k), values_ref[...], ((1,), (1,)))

        @pl.when(k < 3)
        def _():
            transpose_weight(k + 2)

        @pl.when(k >= 2)
        def _():
            transpose_tokens(plane(k - 3))

        return carry

    lax.fori_loop(0, pairs, third_step, 0)

    scale = 1.0 / HS**0.5
    row_id = lax.broadcasted_iota(jnp.int32, (2, length, length), 1)
    col_id = lax.broadcasted_iota(jnp.int32, (2, length, length), 2)
    causal = (col_id <= row_id).reshape(2 * length, length)
    dk_acc[...] = jnp.zeros_like(dk_acc)
    dv_acc[...] = jnp.zeros_like(dv_acc)

    def ag_copy(way, d, k, incoming):
        sign = -1 if way == 0 else 1
        block = dqall.at[k, plane(sign * (d if incoming else d - 1))]
        if d == 4:
            block = block.at[:, pl.ds(way * HS, HS)]
        return remote(block, block, ag_s.at[way, d - 1], ag_r.at[way, d - 1, k], z_up if way == 0 else z_dn)

    def attention_step(k, carry):
        for way in range(2):
            rs_copy(way, 1, k).wait_recv()
        keys = keys_ref[...]
        q = (part[k, z] + ring[0, 0, k] + ring[1, 0, k]).astype(BF16).reshape(2 * length, HS)
        d_probs = d_probs_ref[k]
        scores = jnp.where(causal, dot(q, keys, ((1,), (1,))) * scale, -1e30)
        e = jnp.exp(scores - jnp.max(scores, axis=-1, keepdims=True))
        probs = e * (1.0 / jnp.sum(e, axis=-1, keepdims=True))
        inner = jnp.sum(d_probs * probs, axis=-1, keepdims=True)
        ds = (probs * (d_probs - inner) * scale).astype(BF16)
        dq = dot(ds, keys).astype(BF16)
        dqall[k, z] = jnp.concatenate([dq[:length], dq[length:]], axis=1)
        for way in range(2):
            ag_copy(way, 1, k, False).start()
        low_ref[k], ds_ref[k], q_ref[k] = probs.astype(BF16), ds, q
        return carry

    lax.fori_loop(0, pairs, attention_step, 0)

    def attention_rest(k):
        low, ds, q = low_ref[k], ds_ref[k], q_ref[k]
        ctx = dot(low, values_ref[...]).astype(BF16)
        ctx_ref[:, pair_lanes(k)] = jnp.concatenate([ctx[:length], ctx[length:]], axis=1)
        dv_acc[...] += dot(low, stacked_grads(k), ((0,), (0,)))
        dk_acc[...] += dot(ds, q, ((0,), (0,)))

    groups = [(0, 1), (1, 2), (3, 2), (5, 2), (7, 1)]
    offsets = (0, -1, 1, -2, 2, -3, 3, 4)
    mid = cols // 2

    def y_copy(g, way, d):
        first, count = groups[g]
        slots = pl.ds(first, count)
        if d == 2:
            src = dts.at[slots, y2, :, pl.ds(way * mid, mid)]
            dst = yr2.at[way, slots]
        else:
            src = dts.at[slots, yp if way == 0 else ym]
            dst = yr1.at[way, slots]
        return remote(src, dst, y_s.at[way, d - 1], y_r.at[way, d - 1, g], y_up if way == 0 else y_dn)

    def d_token_block(g, n):
        first, count = groups[g]
        lhs = jnp.concatenate(
            [
                jnp.concatenate([dqall[k, plane(offsets[first + i])] for k in range(pairs)], axis=1)
                for i in range(count)
            ],
            axis=0,
        )
        lanes = pl.ds(pl.multiple_of(n * PW, 128), PW)
        out = dot(lhs, wg_t[:, lanes]).astype(BF16)
        for i in range(count):
            for owner in range(2 * NY):
                block = out[i * length + owner * 16 : i * length + (owner + 1) * 16]
                dts[first + i, owner % NY, (owner // NY) * 16 : (owner // NY + 1) * 16, lanes] = block

    def y_begin(g):
        for way in range(2):
            y_copy(g, way, 2).start()

    def y_first(g):
        first, count = groups[g]
        for way in range(2):
            y_copy(g, way, 2).wait_recv()
            to = yp if way == 0 else ym
            for i in range(count):
                own = dts[first + i, to, :, way * mid : (way + 1) * mid].astype(F32)
                came = yr2[way, first + i].astype(F32)
                dts[first + i, to, :, way * mid : (way + 1) * mid] = (own + came).astype(BF16)
            y_copy(g, way, 1).start()

    batches = [(0, 3), (3, 2), (5, 3)]

    def x_copy(b):
        first, count = batches[b]
        slots = pl.ds(first, count)
        return remote(red.at[slots, 1 - xh], xr.at[slots], x_s, x_r.at[b], other_xh)

    def y_second(g):
        first, count = groups[g]
        for way in range(2):
            y_copy(g, way, 1).wait_recv()
        for i in range(count):
            slot = first + i
            total = dts[slot, y].astype(F32) + yr1[0, slot].astype(F32) + yr1[1, slot].astype(F32)
            for side in range(2):
                red[slot, side] = total[side * 16 : (side + 1) * 16].astype(BF16)

    def home_copy(slot):
        block = dtk.at[:, pl.ds(pl.multiple_of(z * depth, 128), depth)]
        return remote(fin.at[slot], block, zd_s, zd_r.at[slot], at_z(plane(offsets[slot])))

    def home_in(slot):
        block = dtk.at[:, pl.ds(pl.multiple_of(plane(-offsets[slot]) * depth, 128), depth)]
        return remote(fin.at[slot], block, zd_s, zd_r.at[slot], z_up)

    def x_done(b):
        first, count = batches[b]
        x_copy(b).wait_recv()
        for i in range(count):
            slot = first + i
            total = (red[slot, xh].astype(F32) + xr[slot].astype(F32)).astype(BF16)
            if slot == 0:
                dtk[:, pl.ds(pl.multiple_of(z * depth, 128), depth)] = total
            else:
                fin[slot] = total
                home_copy(slot).start()

    def gc_copy(k):
        return remote(gs.at[k], gcr.at[k], gc_s, gc_r.at[k], other_core)

    def gx_copy(k):
        return remote(gxs.at[k], gxr.at[k], gx_s, gx_r.at[k], other_xl)

    def own_rows(side, core):
        return pl.ds(pl.multiple_of((side * 2 + core) * rows, 64), rows)

    def core_sum(k):
        gc_copy(k).wait_recv()
        away = 1 - xl
        gxs[k] = (ga[k, own_rows(away, c), :] + gcr[k, away].astype(F32)).astype(BF16)
        gx_copy(k).start()

    def grad_block(k):
        ga[k] = dot(tok_t[...], dqall[k].reshape(NZ * length, PW))
        for side in range(2):
            gs[k, side] = ga[k, own_rows(side, 1 - c), :].astype(BF16)
        gc_copy(k).start()

    def gather_step(d, k):
        for way in range(2):
            ag_copy(way, d, k, True).wait_recv()
            if d < 4:
                ag_copy(way, d + 1, k, False).start()

    def d_token_blocks(g, low, high):
        def step(n, carry):
            d_token_block(g, n)
            return carry

        lax.fori_loop(low, high, step, 0)

    def grad_done(k):
        gx_copy(k).wait_recv()
        mine = ga[k, own_rows(xl, c), :] + gcr[k, xl].astype(F32) + gxr[k].astype(F32)
        grad_ref[:, k * PW : (k + 1) * PW] = mine

    for k in range(pairs):
        gather_step(1, k)
        d_token_block(0, k)
        if k < 2:
            attention_rest(k)
    y_begin(0)
    d_token_blocks(1, 0, pairs)
    y_begin(1)
    gather_step(2, 0)
    attention_rest(2)
    gather_step(2, 1)
    attention_rest(3)
    gather_step(2, 2)
    attention_rest(4)
    dk_ref[...] = dk_acc[...].astype(BF16)
    dv_ref[...] = dv_acc[...].astype(BF16)
    kept = ((ctx_ref, ctx_hbm), (dk_ref, dk_hbm), (dv_ref, dv_hbm))
    stores = [pltpu.make_async_copy(src, dst, out_sem.at[i]) for i, (src, dst) in enumerate(kept)]
    for store in stores:
        store.start()
    y_first(0)
    gather_step(3, 0)
    gather_step(2, 3)
    gather_step(3, 1)
    gather_step(2, 4)
    d_token_blocks(2, 0, pairs)
    y_begin(2)
    y_first(1)
    gather_step(3, 2)
    gather_step(4, 0)
    grad_block(0)
    y_second(0)
    gather_step(3, 3)
    gather_step(4, 1)
    grad_block(1)
    core_sum(0)
    gather_step(3, 4)
    d_token_blocks(3, 0, pairs)
    y_begin(3)
    y_first(2)
    y_second(1)
    x_copy(0).start()
    gather_step(4, 2)
    gather_step(4, 3)
    gather_step(4, 4)
    d_token_blocks(4, 0, pairs)
    y_begin(4)
    core_sum(1)
    grad_block(2)
    grad_block(3)
    core_sum(2)
    y_second(2)
    x_copy(1).start()
    y_first(3)
    core_sum(3)
    grad_block(4)
    y_first(4)
    core_sum(4)
    y_second(3)
    y_second(4)
    x_copy(2).start()
    x_done(0)
    x_done(1)
    grad_done(0)
    grad_done(1)
    grad_done(2)
    grad_done(3)
    ahead, last = pl.ds(0, cols - PW), pl.ds(cols - PW, PW)
    most_store = pltpu.make_async_copy(grad_ref.at[:, ahead], grad_hbm.at[:, ahead], out_sem.at[3])
    most_store.start()
    x_done(2)
    grad_done(4)
    grad_store = pltpu.make_async_copy(grad_ref.at[:, last], grad_hbm.at[:, last], out_sem.at[5])
    grad_store.start()
    for slot in range(1, NZ):
        home_in(slot).wait_recv()
    dtok_store = pltpu.make_async_copy(dtk, dtok_hbm, out_sem.at[4])
    dtok_store.start()

    def sent(src, sem):
        remote(src, src, sem, gc_r.at[0], other_core).wait_send()

    for j in (3, 5, 6):
        token_out(j).wait_send()
    for kind in range(4):
        sent(tok.at[pl.ds(0, NZ - 1), pl.ds(0, half_rows if kind >= 2 else quarter), :], ty_s.at[kind])
    for kind in range(3):
        sent(wg.at[:, pl.ds(0, rows), :], w_s.at[kind])
    for way in range(2):
        for d in (1, 2, 3):
            sent(part.at[:, 0], rs_s.at[way, d - 1])
            sent(dqall.at[:, 0], ag_s.at[way, d - 1])
        sent(part.at[:, 0, 0], rs_s.at[way, 3])
        sent(dqall.at[:, 0, :, pl.ds(0, HS)], ag_s.at[way, 3])
        sent(dts.at[:, 0], y_s.at[way, 0])
        sent(dts.at[:, 0, :, pl.ds(0, mid)], y_s.at[way, 1])
    sent(fin.at[pl.ds(1, NZ - 1)], zd_s)
    sent(xr, x_s)
    sent(gs, gc_s)
    sent(gxs, gx_s)
    for store in stores + [most_store, grad_store, dtok_store]:
        store.wait()


def fused(tokens, master, keys, values, d_context):
    length, width = tokens.shape
    rows, cols = master.shape
    depth, pairs, mid, quarter = 4 * rows, cols // PW, cols // 2, length // NY
    vmem, dma = pltpu.VMEM, pltpu.SemaphoreType.DMA
    anywhere = pl.BlockSpec(memory_space=pl.ANY)
    return pl.pallas_call(
        kernel,
        out_shape=(
            jax.ShapeDtypeStruct((length, cols), BF16),
            jax.ShapeDtypeStruct((length, HS), BF16),
            jax.ShapeDtypeStruct((length, HS), BF16),
            jax.ShapeDtypeStruct((length // 8, width), BF16),
            jax.ShapeDtypeStruct((rows, cols), F32),
        ),
        in_specs=[anywhere] * 5,
        out_specs=[anywhere] * 5,
        scratch_shapes=[
            vmem((rows, cols), F32),
            vmem((length, HS), BF16),
            vmem((length, HS), BF16),
            vmem((length, cols), BF16),
            vmem((length, cols), BF16),
            vmem((length, HS), BF16),
            vmem((length, HS), BF16),
            vmem((rows, cols), F32),
            vmem((NZ, length, depth), BF16),
            vmem((depth, NZ * length), BF16),
            vmem((pairs, depth, PW), BF16),
            vmem((cols, depth), BF16),
            vmem((pairs, NZ, 2, length, HS), F32),
            vmem((2, 4, pairs, 2, length, HS), F32),
            vmem((pairs, NZ, length, PW), BF16),
            vmem((length, HS), F32),
            vmem((length, HS), F32),
            vmem((pairs, 2 * length, HS), F32),
            vmem((pairs, 2 * length, HS), BF16),
            vmem((pairs, 2 * length, HS), BF16),
            vmem((pairs, 2 * length, HS), BF16),
            vmem((NZ, NY, quarter, depth), BF16),
            vmem((2, NZ, quarter, mid), BF16),
            vmem((2, NZ, quarter, depth), BF16),
            vmem((NZ, 2, 16, depth), BF16),
            vmem((NZ, 16, depth), BF16),
            vmem((NZ, 16, depth), BF16),
            vmem((length // 8, width), BF16),
            vmem((pairs, depth, PW), F32),
            vmem((pairs, 2, rows, PW), BF16),
            vmem((pairs, 2, rows, PW), BF16),
            vmem((pairs, rows, PW), BF16),
            vmem((pairs, rows, PW), BF16),
            dma((4,)),
            dma((6,)),
            dma,
            dma((3,)), dma((3, pairs)),
            dma((NZ - 1,)), dma((NZ - 1,)),
            dma((4,)), dma((4, NZ - 1)),
            dma((2, 4)), dma((2, 4, pairs)),
            dma((2, 4)), dma((2, 4, pairs)),
            dma((2, 2)), dma((2, 2, 5)),
            dma, dma((3,)),
            dma, dma((NZ,)),
            dma, dma((pairs,)),
            dma, dma((pairs,)),
        ],
        compiler_params=pltpu.CompilerParams(
            collective_id=0, has_side_effects=True, vmem_limit_bytes=54 * 1024 * 1024
        ),
    )(tokens, master, keys, values, d_context)


def finish_kernel(*refs):
    wide, small, outs, tidy = refs[:4], refs[4:8], refs[8:11], refs[11:15]
    old, news, held, wide_in, new_out, small_in, small_out = refs[15], refs[16], refs[17:21], *refs[21:]
    parts, rows = old.shape[1], old.shape[2]
    came = [
        [pltpu.make_async_copy(wide[n].at[pl.ds(i * rows, rows)], old.at[n, i], wide_in.at[n, i]) for n in range(4)]
        for i in range(parts)
    ]
    first = [pltpu.make_async_copy(a, b, small_in.at[i]) for i, (a, b) in enumerate(zip(small, held))]
    second = [pltpu.make_async_copy(a, b, small_out.at[i]) for i, (a, b) in enumerate(zip(held, tidy))]
    for copy in came[0] + first + sum(came[1:], []):
        copy.start()
    writes = []
    for i in range(parts):
        for copy in came[i]:
            copy.wait()
        for n, value in enumerate(adam_piece(old[1, i], old[2, i], old[3, i], old[0, i])):
            news[n, i] = value
            writes.append(pltpu.make_async_copy(news.at[n, i], outs[n].at[pl.ds(i * rows, rows)], new_out.at[n, i]))
            writes[-1].start()
        if i == 0:
            for a, b in zip(first, second):
                a.wait()
                b.start()
    for copy in second + writes:
        copy.wait()


def finish(gradient, master, one, two, small):
    rows, cols = master.shape
    parts = 5
    anywhere = pl.BlockSpec(memory_space=pl.ANY)
    vmem, dma = pltpu.VMEM, pltpu.SemaphoreType.DMA
    like = jax.ShapeDtypeStruct((rows, cols), F32)
    return pl.pallas_call(
        finish_kernel,
        out_shape=[like] * 3 + [jax.ShapeDtypeStruct(a.shape, a.dtype) for a in small],
        in_specs=[anywhere] * 8,
        out_specs=[anywhere] * 7,
        scratch_shapes=[vmem((4, parts, rows // parts, cols), F32), vmem((3, parts, rows // parts, cols), F32)]
        + [vmem(a.shape, a.dtype) for a in small]
        + [dma((4, parts)), dma((3, parts)), dma((4,)), dma((4,))],
        compiler_params=pltpu.CompilerParams(vmem_limit_bytes=60 * 1024 * 1024),
    )(gradient, master, one, two, *small)


def body(tokens, master, moment_one, moment_two, keys, values, d_context):
    *small, gradient = fused(tokens, master, keys, values, d_context)
    new_master, new_one, new_two, *small = finish(gradient, master, moment_one, moment_two, small)
    return (*small, new_master, new_one, new_two)


def solution(mesh):
    both = P("node", "local")
    return jax.shard_map(
        body,
        mesh=mesh,
        in_specs=(P("node", None), both, both, both, both, both, both),
        out_specs=(both, both, both, P(("node", "local"), None), both, both, both),
        check_vma=False,
    )
```
